512 devices in a mesh: mem: 8 (over z_lo, core), tile: 64 (over x, y, z_hi).
Axes of the slice: x: 4, y: 8, z: 8 (z_hi: 2, z_lo: 4; z = z_hi * 4 + z_lo), core: 2. Of those that a mesh axis runs over, the one named last changes fastest.
Arguments:
- background: bfloat16 [64, 3, 64, 8192], P('mem', None, None, 'tile'), may hold values from -12 to 12
- obs_value: bfloat16 [64, 8192], P('mem', 'tile'), may hold values from -6 to 6
- obs_var: bfloat16 [64, 8192], P('mem', 'tile'), may hold values from 1 to 16
- obs_index: int32 [8, 512, 256], P('mem', 'tile'), may hold values from 0 to 2175
- ice_mask: int32 [64, 8192], P(None, 'tile'), may hold values 0 or 1
- wind_stress: bfloat16 [2, 64, 8192], P(None, None, 'tile'), may hold values from -3 to 3
Outputs:
- forecast: bfloat16 [64, 3, 64, 8192], P('mem', None, None, 'tile')
The draws below stay inside these ranges and needn't reach their ends.
Inputs may be any that keep to these rules, and one draw needn't show every extreme that they name: Entry k of obs_index[g, p] is the cell r = k // 272, c = k % (272) of the window of row block g and patch p: row g*8+r, column (p*16 - 128+c) mod 8192.
All inputs are finite; a program needn't handle non-finite values. No bound on the sum of `ice_mask` on one device may be relied on, other than what follows from the above.
Results may differ from the reference program's by a relative error of at most 0.0029.
Values may be sent and summed in bfloat16 or wider, within the bound.
A program may use at most 64 MiB of HBM per device.

```python
import math
import jax
import jax.numpy as jnp
from jax import lax

ENS = 64
R = 64
RB = 8
NXC = 8192
PC = 16
NPATCH = 512
W = 128
L = 256
NS_ITERS = 6
N_MEM = 8


def draw_background(key, part):
    key = jax.random.fold_in(key, 11)
    key_scale, key_base, key_mean = jax.random.split(key, 3)
    shape = (ENS, 3, R, NXC)
    member_scale = jnp.exp(jax.random.uniform(key_scale, (ENS, 1, 1, 1), jnp.float32, jnp.log(0.5), jnp.log(2.0)))
    base = jax.random.normal(key_base, shape, jnp.float32)
    common = 0.5 * jax.random.normal(key_mean, (1, 3, R, NXC), jnp.float32)
    value = jnp.clip(common + member_scale * base, -12.0, 12.0)
    return value.astype(jnp.bfloat16)


def with_ends(values, stream_key, low, high):
    longest = values.shape.index(max(values.shape))
    spots = []
    for shift in (0, 1):
        where = [jax.random.randint(jax.random.fold_in(stream_key, axis), (), 0, length) for axis, length in enumerate(values.shape)]
        where[longest] = (where[longest] + shift) % values.shape[longest]
        spots.append(tuple(where))
    return values.at[spots[0]].set(low).at[spots[1]].set(high)


def levels(own_key, dims, cuts, least, largest):
    level = 1.0
    for axis_at, parts in cuts:
        draws = jax.random.uniform(jax.random.fold_in(jax.random.fold_in(own_key, 6), axis_at), (parts,), jnp.float32, least / len(cuts), largest / len(cuts))
        level = level * jnp.repeat(jnp.exp(draws), dims[axis_at] // parts).reshape((-1,) + (1,) * (len(dims) - 1 - axis_at))
    return level


def noise(key, dims, spread, limit, pieces=(), kind=jnp.bfloat16):
    array = spread * jax.random.normal(key, dims, jnp.float32)
    if pieces:
        array = array * levels(key, dims, pieces, -0.22, 0.18)
    return jnp.clip(array, -limit, limit).astype(kind)


def setup_inputs(seed: int = 0) -> dict:
    key_of = jax.random.split(jax.random.key(seed), 7)
    background = draw_background(jax.random.fold_in(key_of[6], 71), 0)
    obs_value = noise(key_of[1], (R, NXC), 1.0, 6.0, ((0, 8), (1, 64)))
    obs_var = jnp.clip(jnp.exp(math.log(16.0) - 2.7725887 * jax.random.uniform(key_of[2], (R, NXC), jnp.float32) ** levels(key_of[2], (R, NXC), ((0, 8), (1, 64)), -0.2, 0.2)), 1.0, 16.0).astype(jnp.bfloat16)
    obs_index = with_ends(jax.random.randint(key_of[3], (N_MEM, NPATCH, L), 0, RB * (PC + 2 * W)), jax.random.fold_in(key_of[3], 1), 0, (RB * (PC + 2 * W)) - 1).astype(jnp.int32)
    ice_mask = with_ends((jax.random.randint(key_of[4], (R, NXC), 0, 4) < 3).astype(jnp.int32), jax.random.fold_in(key_of[4], 1), 0, 1)
    wind_stress = noise(key_of[5], (2, R, NXC), 0.5, 3.0, ((2, 64),))
    return dict(background=background, obs_value=obs_value, obs_var=obs_var, obs_index=obs_index, ice_mask=ice_mask, wind_stress=wind_stress)


STRENGTH = 1.0

def row_slope(field):
    widths = [(0, 0)] * (field.ndim - 2) + [(1, 1), (0, 0)]
    padded = jnp.pad(field, widths)
    return (padded[..., 2:, :] - padded[..., :-2, :]) * 0.5

def column_slope(field):
    return (field[..., 2:] - field[..., :-2]) * 0.5

def new_stress(drift_x, drift_y, first, second, shear, pressure):
    dxx = column_slope(drift_x)
    dyx = column_slope(drift_y)
    dxy = row_slope(drift_x[..., 1:-1])
    dyy = row_slope(drift_y[..., 1:-1])
    first = (first + pressure * (dxx + dyy) - 0.5 * pressure) * 0.5
    second = (second + 0.25 * pressure * (dxx - dyy)) * 0.5
    shear = (shear + 0.25 * pressure * (dxy + dyx)) * 0.5
    return (first, second, shear)

def new_drift(drift_x, drift_y, first, second, shear, mask, tau_x, tau_y):
    normal_x = 0.5 * (first + second)
    normal_y = 0.5 * (first - second)
    force_x = column_slope(normal_x) + row_slope(shear[..., 1:-1])
    force_y = column_slope(shear) + row_slope(normal_y[..., 1:-1])
    drift_x = mask * (drift_x + 0.5 * (force_x + tau_x)) / 1.5
    drift_y = mask * (drift_y + 0.5 * (force_y + tau_y)) / 1.5
    return (drift_x, drift_y)

def wrap_pad(field):
    return jnp.concatenate([field[..., -1:], field, field[..., :1]], axis=-1)

def letkf_weights(ens_obs, obs_y, obs_err):
    members = ens_obs.shape[0]
    hp = lax.Precision.HIGHEST
    obs_mean = lax.optimization_barrier(jnp.mean(ens_obs, axis=0))
    obs_anom = ens_obs - obs_mean
    inverse_var = 1.0 / obs_err
    innovation = obs_y - obs_mean
    identity = jnp.eye(members, dtype=jnp.float32)
    system = jnp.einsum('ipl,jpl->pij', obs_anom * inverse_var, obs_anom, precision=hp)
    system = system + (members - 1.0) * identity
    scale = jnp.sqrt(lax.optimization_barrier(jnp.sum(system * system, axis=(1, 2))))[:, None, None]
    iterate = system / scale
    inverse_root = jnp.broadcast_to(identity, system.shape)
    for sweep in range(NS_ITERS):
        factor = 1.5 * identity - 0.5 * jnp.einsum('pij,pjk->pik', inverse_root, iterate, precision=hp)
        iterate = jnp.einsum('pij,pjk->pik', iterate, factor, precision=hp)
        inverse_root = jnp.einsum('pij,pjk->pik', factor, inverse_root, precision=hp)
    root = inverse_root / jnp.sqrt(scale)
    covariance = jnp.einsum('pij,pjk->pik', root, root, precision=hp)
    projected = jnp.einsum('ipl,pl->pi', obs_anom, inverse_var * innovation, precision=hp)
    mean_weight = jnp.einsum('pij,pj->pi', covariance, projected, precision=hp)
    return jnp.sqrt(members - 1.0) * root + mean_weight[:, :, None]

def reference(background, obs_value, obs_var, obs_index, ice_mask, wind_stress):
    hp = lax.Precision.HIGHEST
    span = PC + 2 * W

    def analyse_block(block):
        start = (block * RB).astype(jnp.int32)
        prior = lax.dynamic_slice_in_dim(background, start, RB, 2).astype(jnp.float32)
        values = lax.dynamic_slice_in_dim(obs_value, start, RB, 0).astype(jnp.float32)
        errors = lax.dynamic_slice_in_dim(obs_var, start, RB, 0).astype(jnp.float32)
        lists = obs_index[block]
        row_of = lists // span
        col_of = lists % span
        patch_start = (jnp.arange(NPATCH, dtype=jnp.int32) * PC)[:, None]
        columns = (patch_start - W + col_of) % NXC
        flat = row_of * NXC + columns
        thick = prior[:, 0].reshape(ENS, RB * NXC)
        ens_obs = jnp.take(thick, flat, axis=1)
        obs_y = jnp.take(values.reshape(-1), flat)
        obs_err = jnp.take(errors.reshape(-1), flat)
        weights = letkf_weights(ens_obs, obs_y, obs_err)
        blocks = prior.reshape(ENS, 3, RB, NPATCH, PC)
        prior_mean = lax.optimization_barrier(jnp.mean(blocks, axis=0))
        anomalies = blocks - prior_mean
        analysed = prior_mean + jnp.einsum('pij,ivrpc->jvrpc', weights, anomalies, precision=hp)
        return analysed.astype(jnp.bfloat16)
    blocks_out = lax.map(analyse_block, jnp.arange(N_MEM, dtype=jnp.int32))
    analysis = jnp.transpose(blocks_out, (1, 2, 0, 3, 4, 5)).reshape(ENS, 3, R, NXC)
    mask = ice_mask.astype(jnp.float32)
    tau = wind_stress.astype(jnp.float32)

    def dynamics(member):
        fields = member.astype(jnp.float32)
        drift_x, drift_y = (fields[1], fields[2])
        pressure = STRENGTH * jax.nn.softplus(fields[0])
        first = jnp.zeros_like(pressure)
        second = jnp.zeros_like(pressure)
        shear = jnp.zeros_like(pressure)
        for sweep in range(2):
            first, second, shear = new_stress(wrap_pad(drift_x), wrap_pad(drift_y), first, second, shear, pressure)
            drift_x, drift_y = new_drift(drift_x, drift_y, wrap_pad(first), wrap_pad(second), wrap_pad(shear), mask, tau[0], tau[1])
        return jnp.stack([member[0], drift_x.astype(jnp.bfloat16), drift_y.astype(jnp.bfloat16)], axis=0)
    return lax.map(dynamics, analysis)
```

```python
import functools

import jax
import jax.numpy as jnp
from jax import lax
from jax.experimental import pallas as pl
from jax.experimental.pallas import tpu as pltpu
from jax.sharding import PartitionSpec as P

F32 = jnp.float32
BF16 = jnp.bfloat16
MESH = pl.DeviceIdType.MESH

ENS = 64
GROUPS = 8
RB = 8
ROWS = 64
PC = 16
W = 128
SPAN = PC + 2 * W
LANES = 128
PATCHES = 8
FIELDS = 3
NS_ITERS = 6
WIDE = PATCHES * ENS
CELLS = 3 * RB * LANES
HALO = 4


def iota(shape, axis):
    return lax.broadcasted_iota(jnp.int32, shape, axis)


def aligned(start, size, by):
    return pl.ds(pl.multiple_of(start, by), size)


def split(x):
    high = x.astype(BF16)
    return high, (x - high.astype(F32)).astype(BF16)


def dot(a, b):
    return jnp.dot(a, b, preferred_element_type=F32)


def dot_lanes(a, b):
    return lax.dot_general(a, b, (((1,), (1,)), ((), ())), preferred_element_type=F32)


def block_diagonal(x):
    segment = iota(x.shape, 1) // ENS
    zero = jnp.zeros_like(x)
    return jnp.concatenate([jnp.where(segment == q, x, zero) for q in range(4)], axis=0)


def patch_products(left, right):
    rows = left.shape[0]
    left_high, left_low = split(left)
    right_high, right_low = split(right)
    out = []
    for half in range(2):
        lanes = slice(half * 256, (half + 1) * 256)
        both = jnp.concatenate([left_high[:, lanes], left_low[:, lanes]], axis=0)
        main = dot(both, block_diagonal(right_high[:, lanes]))
        rest = dot(left_high[:, lanes], block_diagonal(right_low[:, lanes]))
        out.append(main[:rows] + main[rows:] + rest)
    return jnp.concatenate(out, axis=1)


def root_weights(system, projected):
    row = iota((ENS, WIDE), 0)
    eye = ((iota((ENS, WIDE), 1) % ENS) == row).astype(F32)
    full = system + (ENS - 1.0) * eye
    squares = jnp.sum(full * full, axis=0, keepdims=True)
    own = ((iota((PATCHES, WIDE), 1) // ENS) == iota((PATCHES, WIDE), 0)).astype(F32)
    norm = jnp.sum(own * squares, axis=1, keepdims=True)
    scale = jnp.sqrt(jnp.sum(own * norm, axis=0, keepdims=True))
    centring = eye - 1.0 / ENS
    iterate = (system + (ENS - 1.0) * centring) / scale
    factor = 1.5 * eye - 0.5 * iterate
    inverse_root = 1.5 * centring - 0.5 * iterate
    moved = patch_products(jnp.concatenate([iterate, projected], axis=0), factor)
    iterate, projected = moved[:ENS], moved[ENS:]
    for sweep in range(1, NS_ITERS):
        factor = 1.5 * eye - 0.5 * patch_products(inverse_root, iterate)
        if sweep < NS_ITERS - 1:
            moved = patch_products(jnp.concatenate([iterate, inverse_root, projected], axis=0), factor)
            iterate, inverse_root, projected = moved[:ENS], moved[ENS : 2 * ENS], moved[2 * ENS :]
        else:
            moved = patch_products(jnp.concatenate([inverse_root, projected], axis=0), factor)
            inverse_root, projected = moved[:ENS], moved[ENS:]
    mean_weight = patch_products(projected, inverse_root)[:1] / scale
    return jnp.sqrt(ENS - 1.0) * (inverse_root / jnp.sqrt(scale)) + (mean_weight + 1.0 / ENS)


def kernel(
    tiles,
    bg, obs_value, obs_var, obs_index, ice_mask, wind,
    out,
    turned, send_a, send_obs, thick, drift, obs, index,
    count, weight, anom_hi, anom_lo, heavy_hi, heavy_lo, acc,
    masked, packed, edge_send, edge_recv,
    send_c, recv_c, send_e, recv_e,
    send_w, recv_w,
    mask_f, tau_x, tau_y, press, field_x, field_y, normal_x, normal_y, shear, final,
    at_s, at_r, ad_s, ad_r, ob_s, ob_r, b_s, b_r, n_s, n_r, c_s, c_r, e_s, e_r, w_s, w_r,
):
    me, tile = lax.axis_index("mem"), lax.axis_index("tile")
    core, z_lo = me % 2, me // 2
    half, ring = tile % 2, tile // 2
    z = half * 4 + z_lo

    def ring_device(at_z, at_core):
        return ((at_z % 4) * 2 + at_core, ring * 2 + at_z // 4)

    chip_mate = (me + 1 - 2 * core, tile)
    side_mate = (me + 1 - 2 * core, lax.rem(tile + tiles - 2 + 4 * core, tiles))
    left_tile = lax.rem(tile + tiles - 1, tiles)
    right_tile = lax.rem(tile + 1, tiles)
    outer_tile = jnp.where(half == 0, left_tile, right_tile)

    barrier = pltpu.get_barrier_semaphore()

    def greet(step, carry):
        at = lax.rem(z * 2 + core + step, 16)
        pl.semaphore_signal(barrier, inc=1, device_id=ring_device(at // 2, at % 2), device_id_type=MESH)
        return carry

    lax.fori_loop(1, 16, greet, 0)
    pl.semaphore_signal(barrier, inc=1, device_id=side_mate, device_id_type=MESH)
    pl.semaphore_signal(barrier, inc=1, device_id=(me, outer_tile), device_id_type=MESH)

    def turn(v):
        turned[...] = bg[:, v].astype(F32).reshape(GROUPS * ROWS, LANES)
        for g in range(GROUPS):
            for pair in range(RB // 2):
                parts = [turned[pl.ds(g * RB + pair * 2 + h, 8, stride=ROWS), :] for h in range(2)]
                send_a[g, v, pair * 16 : pair * 16 + 16, :] = jnp.concatenate(parts, axis=0).astype(BF16)

    turn(0)
    send_obs[...] = jnp.concatenate([obs_value[...].astype(F32), obs_var[...].astype(F32)], axis=0).astype(BF16)

    lane = iota((RB, LANES), 1)

    def flat_field(f):
        return ice_mask[...].astype(F32) if f == 0 else wind[f - 1].astype(F32)

    low = jnp.zeros((RB, LANES), F32)
    high = jnp.zeros((RB, LANES), F32)
    for f in range(FIELDS):
        whole = flat_field(f)
        for g in range(GROUPS):
            j = f * GROUPS + g
            rows = whole[g * RB : (g + 1) * RB]
            here = (lane // HALO) == j
            low = jnp.where(here, pltpu.roll(rows, (HALO * j) % LANES, 1), low)
            high = jnp.where(here, pltpu.roll(rows, (HALO * j + HALO) % LANES, 1), high)
    send_w[0] = low
    send_w[1] = high

    pl.semaphore_wait(barrier, 17)

    def remote(src, dst, s_sem, r_sem, device):
        return pltpu.make_async_remote_copy(
            src_ref=src, dst_ref=dst, send_sem=s_sem, recv_sem=r_sem, device_id=device, device_id_type=MESH
        )

    def settle(ref, sem):
        pltpu.make_async_copy(ref, ref, sem).wait()

    def send_or_keep(same, src, dst, s_sem, r_sem, device):
        @pl.when(same)
        def _():
            pltpu.make_async_copy(src, dst, r_sem).start()

        @pl.when(jnp.logical_not(same))
        def _():
            remote(src, dst, s_sem, r_sem, device).start()

    def wait_sent(same, src, s_sem):
        @pl.when(jnp.logical_not(same))
        def _():
            settle(src, s_sem)

    at_home = core == half
    for step in (4, 3, 5, 2, 6, 1, 7, 0):
        g = lax.rem(z + step, GROUPS)
        there = ring_device(g, half)
        if step:
            remote(send_a.at[g, 0], thick.at[1, me], at_s.at[step], at_r.at[me], there).start()
        else:
            send_or_keep(at_home, send_a.at[g, 0], thick.at[1, me], at_s.at[step], at_r.at[me], there)
    owner = ring_device(me, half)
    obs_home = jnp.logical_and(owner[0] == me, owner[1] == tile)
    send_or_keep(obs_home, send_obs, obs.at[1], ob_s.at[0], ob_r.at[0], owner)
    send_or_keep(obs_home, obs_index, index, ob_s.at[1], ob_r.at[1], owner)
    remote(send_w.at[0], recv_w.at[1], w_s.at[0], w_r.at[1], (me, left_tile)).start()
    remote(send_w.at[1], recv_w.at[0], w_s.at[1], w_r.at[0], (me, right_tile)).start()

    turn(1)
    turn(2)
    for step in (4, 3, 5, 2, 6, 1, 7, 0):
        g = lax.rem(z + step, GROUPS)
        there = ring_device(g, half)
        if step:
            remote(send_a.at[g, pl.ds(1, 2)], drift.at[me], ad_s.at[step], ad_r.at[me], there).start()
        else:
            send_or_keep(at_home, send_a.at[g, pl.ds(1, 2)], drift.at[me], ad_s.at[step], ad_r.at[me], there)

    settle(index, ob_r.at[1])
    cell = index[...].astype(F32)
    cell_row = jnp.floor((cell + 0.5) * (1.0 / SPAN))
    cell_col = cell - SPAN * cell_row
    row_at = iota((16, cell.shape[1]), 0).astype(F32)
    col_at = iota((3 * LANES, cell.shape[1]), 0).astype(F32)
    for p in range(PATCHES):
        rows = (row_at == cell_row[p : p + 1]).astype(F32).astype(BF16)
        cols = (col_at == cell_col[p : p + 1] + float(p * PC)).astype(F32).astype(BF16)
        hits = dot_lanes(rows, cols)
        for s in range(3):
            count[s, p] = hits[:RB, s * LANES : (s + 1) * LANES]

    settle(obs.at[1], ob_r.at[0])
    mate_slot = 2 * core
    side_slot = 2 - 2 * core
    remote(obs.at[1], obs.at[mate_slot], b_s.at[0, 8], b_r.at[mate_slot, 8], chip_mate).start()
    remote(obs.at[1], obs.at[side_slot], b_s.at[1, 8], b_r.at[side_slot, 8], side_mate).start()
    for j in range(GROUPS):
        settle(thick.at[1, j], at_r.at[j])
        remote(thick.at[1, j], thick.at[side_slot, j], b_s.at[1, j], b_r.at[side_slot, j], side_mate).start()
        remote(thick.at[1, j], thick.at[mate_slot, j], b_s.at[0, j], b_r.at[mate_slot, j], chip_mate).start()

    pad = iota((16, LANES), 0)

    def system_part(s, place):
        both = obs[s].astype(F32)
        values, variance = both[:RB], both[RB:]
        for p in range(PATCHES):
            weight[p] = count[s, p] / variance
        acc_values = values

        def rows_pair(pair, carry):
            two = thick[s, :, aligned(pair * 16, 16, 16), :].astype(F32)
            for h in range(2):
                r = pair * 2 + h
                x = two[:, h * 8 : h * 8 + 8, :].reshape(ENS, LANES)
                mean = jnp.sum(x, axis=0, keepdims=True) * (1.0 / ENS)
                anom = x - mean
                value = jnp.sum(jnp.where(iota((RB, LANES), 0) == r, acc_values, 0.0), axis=0, keepdims=True)
                extra = jnp.where(pad == 0, value - mean, 0.0)
                lanes = aligned((place * RB + r) * LANES, LANES, LANES)
                ext_hi, ext_lo = split(jnp.concatenate([anom, extra], axis=0))
                anom_hi[:, lanes] = ext_hi
                anom_lo[:, lanes] = ext_lo
                for p in range(PATCHES):
                    high, low = split(anom * weight[p, pl.ds(r, 1), :])
                    heavy_hi[p * ENS : (p + 1) * ENS, lanes] = high
                    heavy_lo[p * ENS : (p + 1) * ENS, lanes] = low
            return carry

        lax.fori_loop(0, RB // 2, rows_pair, 0)
        span = slice(place * RB * LANES, (place + 1) * RB * LANES)
        left = jnp.concatenate([anom_hi[:, span], anom_lo[:, span]], axis=0)
        main = dot_lanes(left, heavy_hi[:, span])
        rest = dot_lanes(anom_hi[:, span], heavy_lo[:, span])
        part = main[:80] + main[80:] + rest
        if place == 0:
            acc[...] = part
        else:
            acc[...] += part

    system_part(1, 0)
    for place, s in ((1, 2 - 2 * core), (2, 2 * core)):
        settle(obs.at[s], b_r.at[s, 8])
        for j in range(GROUPS):
            settle(thick.at[s, j], b_r.at[s, j])
        system_part(s, place)

    for j in range(GROUPS):
        settle(drift.at[j], ad_r.at[j])
    edge_lane = iota((ENS, LANES), 1)
    for v in range(FIELDS):
        for pair in range(RB // 2):
            rows = slice(pair * 16, pair * 16 + 16)
            two = (thick[1, :, rows, :] if v == 0 else drift[:, v - 1, rows, :]).astype(F32)
            for h in range(2):
                j = v * RB + pair * 2 + h
                x = two[:, h * 8 : h * 8 + 8, :].reshape(ENS, LANES)
                here = (edge_lane // HALO) == j
                low = pltpu.roll(x, (HALO * j) % LANES, 1)
                high = pltpu.roll(x, (HALO * j + HALO) % LANES, 1)
                if j == 0:
                    packed[0] = jnp.where(here, low, 0.0)
                    packed[1] = jnp.where(here, high, 0.0)
                else:
                    packed[0] = jnp.where(here, low, packed[0])
                    packed[1] = jnp.where(here, high, packed[1])
                for p in range(PATCHES):
                    masked[p * ENS : (p + 1) * ENS, j * LANES : (j + 1) * LANES] = jnp.where(
                        edge_lane // PC == p, x, 0.0
                    ).astype(BF16)

    weights = root_weights(acc[:ENS], acc[ENS:])
    left = jnp.concatenate(split(weights), axis=0)

    for side, p in ((0, 0), (1, PATCHES - 1)):
        edge = dot(left[:, p * ENS : (p + 1) * ENS], packed[side].astype(BF16))
        edge_send[side] = (edge[:ENS] + edge[ENS:]).astype(BF16)
    remote(edge_send.at[1 - core], edge_recv.at[core], n_s.at[0], n_r.at[core], chip_mate).start()
    remote(edge_send.at[core], edge_recv.at[1 - core], n_s.at[1], n_r.at[1 - core], side_mate).start()

    def member_device(step):
        to = lax.rem(me + step, GROUPS)
        return to, (to, ring * 2 + core)

    for v in range(FIELDS):
        for pair in range(RB // 2):
            at = (v * RB + pair * 2) * LANES
            got = dot(left, masked[:, at : at + 256])
            got = got[:ENS] + got[ENS:]
            for to in range(GROUPS):
                rows = slice(to * 8, to * 8 + 8)
                send_c[v, to, pair * 16 : pair * 16 + 16, :] = jnp.concatenate(
                    [got[rows, :LANES], got[rows, LANES:]], axis=0
                ).astype(BF16)
        for step in (4, 3, 5, 2, 6, 1, 7, 0):
            to, there = member_device(step)
            if step:
                remote(send_c.at[v, to], recv_c.at[v, z], c_s.at[v, step], c_r.at[v, z], there).start()
            else:
                send_or_keep(at_home, send_c.at[v, to], recv_c.at[v, z], c_s.at[v, step], c_r.at[v, z], there)
        if v == 1:
            for side in range(2):
                settle(edge_recv.at[side], n_r.at[side])
            for to in range(GROUPS):
                rows = slice(to * 8, to * 8 + 8)
                send_e[to] = jnp.concatenate(
                    [edge_recv[0].astype(F32)[rows], edge_recv[1].astype(F32)[rows]], axis=0
                ).astype(BF16)
            for step in (4, 3, 5, 2, 6, 1, 7, 0):
                to, there = member_device(step)
                if step:
                    remote(send_e.at[to], recv_e.at[z], e_s.at[step], e_r.at[z], there).start()
                else:
                    send_or_keep(at_home, send_e.at[to], recv_e.at[z], e_s.at[step], e_r.at[z], there)

    def strip(own, from_left, from_right, j):
        left_part = pltpu.roll(from_left, (LANES - HALO - HALO * j) % LANES, 1)
        right_part = pltpu.roll(from_right, (64 - HALO * j) % LANES, 1)
        outer = jnp.where(lane >= LANES - HALO, left_part, jnp.where(lane >= 64, right_part, pltpu.roll(own, 64, 1)))
        return jnp.where(lane < 2 * HALO, own, jnp.where(jnp.logical_and(lane >= 68, lane < 124), 0.0, outer))

    for side in range(2):
        settle(recv_w.at[side], w_r.at[side])
    for f, ref in ((0, mask_f), (1, tau_x), (2, tau_y)):
        whole = flat_field(f)
        if f == 0:
            whole = whole * (1.0 / 1.5)
        for g in range(GROUPS):
            own = whole[g * RB : (g + 1) * RB]
            gain = 1.0 / 1.5 if f == 0 else 1.0
            edges = strip(own, recv_w[0] * gain, recv_w[1] * gain, f * GROUPS + g)
            for r in range(RB):
                row = (g * RB + r) * 16
                ref[row : row + 8, :] = jnp.broadcast_to(own[r : r + 1], (8, LANES))
                ref[row + 8 : row + 16, :] = jnp.broadcast_to(edges[r : r + 1], (8, LANES))

    for ref in (field_x, field_y, normal_x, normal_y, shear):
        ref[0:16, :] = jnp.zeros((16, LANES), F32)
        ref[(ROWS + 1) * 16 :, :] = jnp.zeros((16, LANES), F32)

    for g in range(GROUPS):
        settle(recv_e.at[g], e_r.at[g])
        for v in range(FIELDS):
            settle(recv_c.at[v, g], c_r.at[v, g])

    def unpack(g, carry):
        edges = recv_e[g].astype(F32)
        for v in range(FIELDS):
            for pair in range(RB // 2):
                two = recv_c[v, g, pair * 16 : pair * 16 + 16, :].astype(F32)
                if v == 0:
                    final[0, aligned(g * 64 + pair * 16, 16, 16), :] = two
                for h in range(2):
                    r = pair * 2 + h
                    own = two[h * 8 : h * 8 + 8]
                    both = jnp.concatenate([own, strip(own, edges[:8], edges[8:], v * RB + r)], axis=0)
                    row = g * RB + r
                    if v == 0:
                        soft = jnp.maximum(both, 0.0) + jnp.log1p(jnp.exp(-jnp.abs(both)))
                        press[aligned(row * 16, 16, 16), :] = soft
                    else:
                        (field_x, field_y)[v - 1][aligned((row + 1) * 16, 16, 16), :] = both
        return carry

    lax.fori_loop(0, GROUPS, unpack, 0)

    block = 4

    def around(ref, at):
        start = at * block * 16
        return [ref[aligned(start + 16 * k, block * 16, 16), :] for k in range(3)]

    def slope_x(x):
        return 0.5 * (pltpu.roll(x, LANES - 1, 1) - pltpu.roll(x, 1, 1))

    for sweep in range(2):

        def stress(at, carry):
            x_up, x, x_down = around(field_x, at)
            y_up, y, y_down = around(field_y, at)
            p = press[aligned(at * block * 16, block * 16, 16), :]
            here = aligned((at * block + 1) * 16, block * 16, 16)
            dxx, dyx = slope_x(x), slope_x(y)
            dxy, dyy = 0.5 * (x_down - x_up), 0.5 * (y_down - y_up)
            half_p = 0.5 * p
            spread = half_p * (dxx + dyy) - 0.5 * half_p
            skew = (0.25 * half_p) * (dxx - dyy)
            turn_rate = (0.25 * p) * (dxy + dyx)
            new = (spread + skew, spread - skew, turn_rate)
            for ref, term in zip((normal_x, normal_y, shear), new):
                ref[here, :] = 0.5 * term if sweep == 0 else 0.5 * (ref[here, :] + term)
            return carry

        lax.fori_loop(0, ROWS // block, stress, 0)

        def move(at, carry):
            s_up, s, s_down = around(shear, at)
            n_up, _, n_down = around(normal_y, at)
            here = aligned((at * block + 1) * 16, block * 16, 16)
            flat = aligned(at * block * 16, block * 16, 16)
            free = mask_f[flat, :]
            force_x = slope_x(normal_x[here, :]) + 0.5 * (s_down - s_up) + tau_x[flat, :]
            force_y = slope_x(s) + 0.5 * (n_down - n_up) + tau_y[flat, :]
            new_x = free * (field_x[here, :] + 0.5 * force_x)
            new_y = free * (field_y[here, :] + 0.5 * force_y)
            if sweep == 0:
                field_x[here, :] = new_x
                field_y[here, :] = new_y
            else:
                for v, new in ((1, new_x), (2, new_y)):
                    new = new.reshape(block, 16, LANES)
                    main = new[:, :8].reshape(block * 8, LANES)
                    edge = new[:, 8:].reshape(block * 8, LANES)
                    at_lane = iota((block * 8, LANES), 1)
                    main = jnp.where(at_lane < HALO, edge, main)
                    main = jnp.where(at_lane >= LANES - HALO, pltpu.roll(edge, 64, 1), main)
                    final[v, aligned(at * block * 8, block * 8, 8), :] = main
            return carry

        lax.fori_loop(0, ROWS // block, move, 0)

    for v in range(FIELDS):
        for j in range(GROUPS):
            for start in range(0, ROWS, 16):
                parts = [final[v, pl.ds((start + h * 8) * 8 + j, 8, stride=8), :] for h in range(2)]
                out[j, v, start : start + 16, :] = jnp.concatenate(parts, axis=0).astype(BF16)

    for step in range(GROUPS):
        g = lax.rem(z + step, GROUPS)
        same = at_home if step == 0 else False
        to, _ = member_device(step)
        pairs = [(send_a.at[g, 0], at_s.at[step]), (send_a.at[g, pl.ds(1, 2)], ad_s.at[step]), (send_e.at[to], e_s.at[step])]
        pairs += [(send_c.at[v, to], c_s.at[v, step]) for v in range(FIELDS)]
        for src, sem in pairs:
            if step == 0:
                wait_sent(at_home, src, sem)
            else:
                settle(src, sem)
    wait_sent(obs_home, send_obs, ob_s.at[0])
    wait_sent(obs_home, obs_index, ob_s.at[1])
    for side in range(2):
        settle(send_w.at[side], w_s.at[side])
        settle(obs.at[1], b_s.at[side, 8])
        settle(edge_send.at[side], n_s.at[side])
        for j in range(GROUPS):
            settle(thick.at[1, j], b_s.at[side, j])


def body(tiles, background, obs_value, obs_var, obs_index, ice_mask, wind_stress):
    vmem = pl.BlockSpec(memory_space=pltpu.VMEM)
    dma = pltpu.SemaphoreType.DMA
    rows = (ROWS + 2) * 16
    return pl.pallas_call(
        functools.partial(kernel, tiles),
        out_shape=jax.ShapeDtypeStruct(background.shape, BF16),
        in_specs=[vmem] * 6,
        out_specs=vmem,
        scratch_shapes=[
            pltpu.VMEM((GROUPS * ROWS, LANES), F32),
            pltpu.VMEM((GROUPS, FIELDS, 64, LANES), BF16),
            pltpu.VMEM((16, LANES), BF16),
            pltpu.VMEM((3, GROUPS, 64, LANES), BF16),
            pltpu.VMEM((GROUPS, 2, 64, LANES), BF16),
            pltpu.VMEM((3, 16, LANES), BF16),
            pltpu.VMEM((PATCHES, obs_index.shape[2]), jnp.int32),
            pltpu.VMEM((3, PATCHES, RB, LANES), F32),
            pltpu.VMEM((PATCHES, RB, LANES), F32),
            pltpu.VMEM((80, CELLS), BF16),
            pltpu.VMEM((80, CELLS), BF16),
            pltpu.VMEM((WIDE, CELLS), BF16),
            pltpu.VMEM((WIDE, CELLS), BF16),
            pltpu.VMEM((80, WIDE), F32),
            pltpu.VMEM((WIDE, FIELDS * RB * LANES), BF16),
            pltpu.VMEM((2, ENS, LANES), F32),
            pltpu.VMEM((2, ENS, LANES), BF16),
            pltpu.VMEM((2, ENS, LANES), BF16),
            pltpu.VMEM((FIELDS, GROUPS, 64, LANES), BF16),
            pltpu.VMEM((FIELDS, GROUPS, 64, LANES), BF16),
            pltpu.VMEM((GROUPS, 16, LANES), BF16),
            pltpu.VMEM((GROUPS, 16, LANES), BF16),
            pltpu.VMEM((2, RB, LANES), F32),
            pltpu.VMEM((2, RB, LANES), F32),
            pltpu.VMEM((ROWS * 16, LANES), F32),
            pltpu.VMEM((ROWS * 16, LANES), F32),
            pltpu.VMEM((ROWS * 16, LANES), F32),
            pltpu.VMEM((ROWS * 16, LANES), F32),
            pltpu.VMEM((rows, LANES), F32),
            pltpu.VMEM((rows, LANES), F32),
            pltpu.VMEM((rows, LANES), F32),
            pltpu.VMEM((rows, LANES), F32),
            pltpu.VMEM((rows, LANES), F32),
            pltpu.VMEM((FIELDS, ROWS * 8, LANES), F32),
            dma((GROUPS,)), dma((GROUPS,)),
            dma((GROUPS,)), dma((GROUPS,)),
            dma((2,)), dma((2,)),
            dma((2, 9)), dma((3, 9)),
            dma((2,)), dma((2,)),
            dma((FIELDS, GROUPS)), dma((FIELDS, GROUPS)),
            dma((GROUPS,)), dma((GROUPS,)),
            dma((2,)), dma((2,)),
        ],
        compiler_params=pltpu.CompilerParams(
            collective_id=0, has_side_effects=True, vmem_limit_bytes=50 * 1024 * 1024
        ),
        name="analysis_and_drift",
    )(background, obs_value, obs_var, obs_index[0], ice_mask, wind_stress)


def solution(mesh):
    placed = (
        P("mem", None, None, "tile"),
        P("mem", "tile"),
        P("mem", "tile"),
        P("mem", "tile", None),
        P(None, "tile"),
        P(None, None, "tile"),
    )
    return jax.shard_map(
        functools.partial(body, mesh.shape["tile"]),
        mesh=mesh,
        in_specs=placed,
        out_specs=P("mem", None, None, "tile"),
        check_vma=False,
    )
```

```python
import functools

import jax
import jax.numpy as jnp
from jax import lax
from jax.experimental import pallas as pl
from jax.experimental.pallas import tpu as pltpu
from jax.sharding import PartitionSpec as P

F32 = jnp.float32
BF16 = jnp.bfloat16
MESH = pl.DeviceIdType.MESH

ENS = 64
GROUPS = 8
RB = 8
ROWS = 64
PC = 16
W = 128
SPAN = PC + 2 * W
LANES = 128
PATCHES = 8
FIELDS = 3
NS_ITERS = 6
WIDE = PATCHES * ENS
CELLS = 3 * RB * LANES
HALO = 4
EDGE_ROWS = 4
STRIP_ROWS = 16 + 2 * EDGE_ROWS


def iota(shape, axis):
    return lax.broadcasted_iota(jnp.int32, shape, axis)


def aligned(start, size, by):
    return pl.ds(pl.multiple_of(start, by), size)


def split(x):
    high = x.astype(BF16)
    return high, (x - high.astype(F32)).astype(BF16)


def dot(a, b):
    return jnp.dot(a, b, preferred_element_type=F32)


def dot_lanes(a, b):
    return lax.dot_general(a, b, (((1,), (1,)), ((), ())), preferred_element_type=F32)


def block_diagonal(x):
    segment = iota(x.shape, 1) // ENS
    zero = jnp.zeros_like(x)
    return jnp.concatenate([jnp.where(segment == q, x, zero) for q in range(4)], axis=0)


def patch_products(left, right):
    rows = left.shape[0]
    left_high, left_low = split(left)
    right_high, right_low = split(right)
    out = []
    for half in range(2):
        lanes = slice(half * 256, (half + 1) * 256)
        both = jnp.concatenate([left_high[:, lanes], left_low[:, lanes]], axis=0)
        main = dot(both, block_diagonal(right_high[:, lanes]))
        rest = dot(left_high[:, lanes], block_diagonal(right_low[:, lanes]))
        out.append(main[:rows] + main[rows:] + rest)
    return jnp.concatenate(out, axis=1)


def root_weights(system, projected):
    row = iota((ENS, WIDE), 0)
    eye = ((iota((ENS, WIDE), 1) % ENS) == row).astype(F32)
    full = system + (ENS - 1.0) * eye
    squares = jnp.sum(full * full, axis=0, keepdims=True)
    own = ((iota((PATCHES, WIDE), 1) // ENS) == iota((PATCHES, WIDE), 0)).astype(F32)
    norm = jnp.sum(own * squares, axis=1, keepdims=True)
    scale = jnp.sqrt(jnp.sum(own * norm, axis=0, keepdims=True))
    centring = eye - 1.0 / ENS
    iterate = (system + (ENS - 1.0) * centring) / scale
    factor = 1.5 * eye - 0.5 * iterate
    inverse_root = 1.5 * centring - 0.5 * iterate
    moved = patch_products(jnp.concatenate([iterate, projected], axis=0), factor)
    iterate, projected = moved[:ENS], moved[ENS:]
    for sweep in range(1, NS_ITERS):
        factor = 1.5 * eye - 0.5 * patch_products(inverse_root, iterate)
        if sweep < NS_ITERS - 1:
            moved = patch_products(jnp.concatenate([iterate, inverse_root, projected], axis=0), factor)
            iterate, inverse_root, projected = moved[:ENS], moved[ENS : 2 * ENS], moved[2 * ENS :]
        else:
            moved = patch_products(jnp.concatenate([inverse_root, projected], axis=0), factor)
            inverse_root, projected = moved[:ENS], moved[ENS:]
    mean_weight = patch_products(projected, inverse_root)[:1] / scale
    return jnp.sqrt(ENS - 1.0) * (inverse_root / jnp.sqrt(scale)) + (mean_weight + 1.0 / ENS)


def kernel(
    tiles,
    prior, obs_value_hbm, obs_var_hbm, obs_index, mask_hbm, wind_hbm,
    out_hbm,
    obs_value, obs_var, ice_mask, wind,
    tall, send_obs, thick, drift, obs, index,
    count, weight, anom_hi, anom_lo, heavy_hi, heavy_lo, acc,
    masked, packed, edge_send, edge_recv,
    send_c, recv_c, send_e, recv_e,
    send_w, recv_w, padded, flat_halo, strip_halo,
    free, tau_x, tau_y, press, field_x, field_y, normal_x, normal_y, shear,
    strip_free, strip_tau_x, strip_tau_y, strip_press, strip_x, strip_y, strip_normal_x, strip_normal_y, strip_shear,
    final, result,
    in_s, out_s, at_s, at_r, ad_s, ad_r, ob_s, ob_r, b_s, b_r, n_s, n_r, c_s, c_r, e_s, e_r, w_s, w_r,
):
    me, tile = lax.axis_index("mem"), lax.axis_index("tile")
    core, z_lo = me % 2, me // 2
    half, ring = tile % 2, tile // 2
    z = half * 4 + z_lo

    def ring_device(at_z, at_core):
        return ((at_z % 4) * 2 + at_core, ring * 2 + at_z // 4)

    chip_mate = (me + 1 - 2 * core, tile)
    side_mate = (me + 1 - 2 * core, lax.rem(tile + tiles - 2 + 4 * core, tiles))
    left_tile = lax.rem(tile + tiles - 1, tiles)
    right_tile = lax.rem(tile + 1, tiles)
    outer_tile = jnp.where(half == 0, left_tile, right_tile)

    loads = [
        pltpu.make_async_copy(src, dst, in_s.at[i])
        for i, (src, dst) in enumerate(
            (
                (obs_value_hbm, obs_value),
                (obs_var_hbm, obs_var),
                (mask_hbm, ice_mask),
                (wind_hbm, wind),
            )
        )
    ]
    for load in loads:
        load.start()

    barrier = pltpu.get_barrier_semaphore()

    def greet(step, carry):
        at = lax.rem(z * 2 + core + lax.rem(step + 7, 15) + 1, 16)
        pl.semaphore_signal(barrier, inc=1, device_id=ring_device(at // 2, at % 2), device_id_type=MESH)
        return carry

    lax.fori_loop(1, 16, greet, 0)
    pl.semaphore_signal(barrier, inc=1, device_id=side_mate, device_id_type=MESH)
    pl.semaphore_signal(barrier, inc=1, device_id=(me, outer_tile), device_id_type=MESH)

    lane = iota((RB, LANES), 1)

    pl.semaphore_wait(barrier, 17)

    def remote(src, dst, s_sem, r_sem, device):
        return pltpu.make_async_remote_copy(
            src_ref=src, dst_ref=dst, send_sem=s_sem, recv_sem=r_sem, device_id=device, device_id_type=MESH
        )

    def settle(ref, sem):
        pltpu.make_async_copy(ref, ref, sem).wait()

    def send_or_keep(same, src, dst, s_sem, r_sem, device):
        @pl.when(same)
        def _():
            pltpu.make_async_copy(src, dst, r_sem).start()

        @pl.when(jnp.logical_not(same))
        def _():
            remote(src, dst, s_sem, r_sem, device).start()

    def wait_sent(same, src, s_sem):
        @pl.when(jnp.logical_not(same))
        def _():
            settle(src, s_sem)

    at_home = core == half
    far_first = (4, 3, 5, 2, 6, 1, 7, 0)
    for step in far_first:
        g = lax.rem(z + step, GROUPS)
        there = ring_device(g, half)
        if step:
            remote(prior.at[:, 0, g], thick.at[1, me], at_s.at[step], at_r.at[me], there).start()
        else:
            send_or_keep(at_home, prior.at[:, 0, g], thick.at[1, me], at_s.at[step], at_r.at[me], there)
    owner = ring_device(me, half)
    obs_home = jnp.logical_and(owner[0] == me, owner[1] == tile)
    send_or_keep(obs_home, obs_index, index, ob_s.at[1], ob_r.at[1], owner)
    for load in loads:
        load.wait()
    send_obs[...] = jnp.concatenate([obs_value[...].astype(F32), obs_var[...].astype(F32)], axis=0).astype(BF16)
    send_or_keep(obs_home, send_obs, obs.at[1], ob_s.at[0], ob_r.at[0], owner)
    def flat_field(f):
        return ice_mask[...].astype(F32) if f == 0 else wind[f - 1].astype(F32)

    low = jnp.zeros((RB, LANES), F32)
    high = jnp.zeros((RB, LANES), F32)
    for f in range(FIELDS):
        whole = flat_field(f)
        for g in range(GROUPS):
            j = f * GROUPS + g
            rows = whole[g * RB : (g + 1) * RB]
            here = (lane // HALO) == j
            low = jnp.where(here, pltpu.roll(rows, (HALO * j) % LANES, 1), low)
            high = jnp.where(here, pltpu.roll(rows, (HALO * j + HALO) % LANES, 1), high)
    send_w[0] = low
    send_w[1] = high

    remote(send_w.at[0], recv_w.at[1], w_s.at[0], w_r.at[1], (me, left_tile)).start()
    remote(send_w.at[1], recv_w.at[0], w_s.at[1], w_r.at[0], (me, right_tile)).start()

    settle(index, ob_r.at[1])
    cell = index[...].astype(F32)
    cell_row = jnp.floor((cell + 0.5) * (1.0 / SPAN))
    cell_col = cell - SPAN * cell_row
    row_at = iota((16, cell.shape[1]), 0).astype(F32)
    col_at = iota((3 * LANES, cell.shape[1]), 0).astype(F32)
    for p in range(PATCHES):
        rows = (row_at == cell_row[p : p + 1]).astype(F32).astype(BF16)
        cols = (col_at == cell_col[p : p + 1] + float(p * PC)).astype(F32).astype(BF16)
        hits = dot_lanes(rows, cols)
        for s in range(3):
            count[s, p] = hits[:RB, s * LANES : (s + 1) * LANES]

    settle(obs.at[1], ob_r.at[0])
    mate_slot = 2 * core
    side_slot = 2 - 2 * core
    remote(obs.at[1], obs.at[mate_slot], b_s.at[0, 8], b_r.at[mate_slot, 8], chip_mate).start()
    remote(obs.at[1], obs.at[side_slot], b_s.at[1, 8], b_r.at[side_slot, 8], side_mate).start()
    for j in range(GROUPS):
        settle(thick.at[1, j], at_r.at[j])
        remote(thick.at[1, j], thick.at[side_slot, j], b_s.at[1, j], b_r.at[side_slot, j], side_mate).start()
        remote(thick.at[1, j], thick.at[mate_slot, j], b_s.at[0, j], b_r.at[mate_slot, j], chip_mate).start()

    for step in far_first:
        g = lax.rem(z + step, GROUPS)
        there = ring_device(g, half)
        if step:
            remote(prior.at[:, pl.ds(1, 2), g], drift.at[me], ad_s.at[step], ad_r.at[me], there).start()
        else:
            send_or_keep(at_home, prior.at[:, pl.ds(1, 2), g], drift.at[me], ad_s.at[step], ad_r.at[me], there)

    pad = iota((16, LANES), 0)

    def system_part(s, place):
        both = obs[s].astype(F32)
        values, variance = both[:RB], both[RB:]
        for p in range(PATCHES):
            weight[p] = count[s, p] / variance
        tall[place] = thick[s].astype(F32).reshape(ENS * RB, LANES)

        def rows_pair(pair, carry):
            for h in range(2):
                r = pair * 2 + h
                x = tall[place, pl.ds(r, ENS, stride=RB), :]
                mean = jnp.sum(x, axis=0, keepdims=True) * (1.0 / ENS)
                anom = x - mean
                value = jnp.sum(jnp.where(iota((RB, LANES), 0) == r, values, 0.0), axis=0, keepdims=True)
                extra = jnp.where(pad == 0, value - mean, 0.0)
                lanes = aligned((place * RB + r) * LANES, LANES, LANES)
                ext_hi, ext_lo = split(jnp.concatenate([anom, extra], axis=0))
                anom_hi[:, lanes] = ext_hi
                anom_lo[:, lanes] = ext_lo
                for p in range(PATCHES):
                    high, low = split(anom * weight[p, pl.ds(r, 1), :])
                    heavy_hi[p * ENS : (p + 1) * ENS, lanes] = high
                    heavy_lo[p * ENS : (p + 1) * ENS, lanes] = low
            return carry

        lax.fori_loop(0, RB // 2, rows_pair, 0)
        span = slice(place * RB * LANES, (place + 1) * RB * LANES)
        left = jnp.concatenate([anom_hi[:, span], anom_lo[:, span]], axis=0)
        main = dot_lanes(left, heavy_hi[:, span])
        rest = dot_lanes(anom_hi[:, span], heavy_lo[:, span])
        part = main[:80] + main[80:] + rest
        if place == 0:
            acc[...] = part
        else:
            acc[...] += part

    system_part(1, 0)
    for place, s in ((1, 2 - 2 * core), (2, 2 * core)):
        settle(obs.at[s], b_r.at[s, 8])
        for j in range(GROUPS):
            settle(thick.at[s, j], b_r.at[s, j])
        system_part(s, place)

    edge_lane = iota((ENS, LANES), 1)

    def spread(v):
        for r in range(RB):
            j = v * RB + r
            x = tall[v, pl.ds(r, ENS, stride=RB), :]
            here = (edge_lane // HALO) == j
            low = pltpu.roll(x, (HALO * j) % LANES, 1)
            high = pltpu.roll(x, (HALO * j + HALO) % LANES, 1)
            if j == 0:
                packed[0] = jnp.where(here, low, 0.0)
                packed[1] = jnp.where(here, high, 0.0)
            else:
                packed[0] = jnp.where(here, low, packed[0])
                packed[1] = jnp.where(here, high, packed[1])
            for p in range(PATCHES):
                masked[p * ENS : (p + 1) * ENS, j * LANES : (j + 1) * LANES] = jnp.where(
                    edge_lane // PC == p, x, 0.0
                ).astype(BF16)

    spread(0)
    weights = root_weights(acc[:ENS], acc[ENS:])
    left = jnp.concatenate(split(weights), axis=0)

    def member_device(step):
        to = lax.rem(me + step, GROUPS)
        return to, (to, ring * 2 + core)

    for v in range(FIELDS):
        if v == 1:
            for j in range(GROUPS):
                settle(drift.at[j], ad_r.at[j])
            for f in (1, 2):
                tall[f] = drift[:, :, f - 1].astype(F32).reshape(ENS * RB, LANES)
                spread(f)
            for side, p in ((0, 0), (1, PATCHES - 1)):
                edge = dot(left[:, p * ENS : (p + 1) * ENS], packed[side].astype(BF16))
                edge_send[side] = (edge[:ENS] + edge[ENS:]).astype(BF16)
            remote(edge_send.at[1 - core], edge_recv.at[core], n_s.at[0], n_r.at[core], chip_mate).start()
            remote(edge_send.at[core], edge_recv.at[1 - core], n_s.at[1], n_r.at[1 - core], side_mate).start()
        if v == 2:
            for side in range(2):
                settle(edge_recv.at[side], n_r.at[side])
            for to in range(GROUPS):
                rows = slice(to * 8, to * 8 + 8)
                send_e[to] = jnp.concatenate(
                    [edge_recv[0].astype(F32)[rows], edge_recv[1].astype(F32)[rows]], axis=0
                ).astype(BF16)
            for step in far_first:
                to, there = member_device(step)
                if step:
                    remote(send_e.at[to], recv_e.at[z], e_s.at[step], e_r.at[z], there).start()
                else:
                    send_or_keep(at_home, send_e.at[to], recv_e.at[z], e_s.at[step], e_r.at[z], there)
        for pair in range(RB // 2):
            at = (v * RB + pair * 2) * LANES
            got = dot(left, masked[:, at : at + 256])
            got = got[:ENS] + got[ENS:]
            for to in range(GROUPS):
                rows = slice(to * 8, to * 8 + 8)
                send_c[v, to, pair * 16 : pair * 16 + 16, :] = jnp.concatenate(
                    [got[rows, :LANES], got[rows, LANES:]], axis=0
                ).astype(BF16)
        for step in far_first:
            to, there = member_device(step)
            if step:
                remote(send_c.at[v, to], recv_c.at[v, aligned(EDGE_ROWS * 8 + z * 64, 64, 16)], c_s.at[v, step], c_r.at[v, z], there).start()
            else:
                send_or_keep(at_home, send_c.at[v, to], recv_c.at[v, aligned(EDGE_ROWS * 8 + z * 64, 64, 16)], c_s.at[v, step], c_r.at[v, z], there)
    at_lane = iota((8, LANES), 1)
    lane_group, lane_in = at_lane // 32, at_lane % 32
    is_right = jnp.logical_and(lane_in >= 8, lane_in < 12)
    is_left = jnp.logical_and(lane_in >= 12, lane_in < 16)

    def strip_edges(from_left, from_right, j, q):
        left_part = pltpu.roll(from_left, (32 * q + 12 - HALO * j) % LANES, 1)
        right_part = pltpu.roll(from_right, (32 * q + 8 - HALO * j) % LANES, 1)
        here = lane_group == q
        part = jnp.where(jnp.logical_and(here, is_left), left_part, 0.0)
        return jnp.where(jnp.logical_and(here, is_right), right_part, part)

    pick_row, pick_lane = iota((4 * LANES, LANES), 0), iota((4 * LANES, LANES), 1)
    pick_col, pick_in = pick_row % LANES, pick_lane % 32
    wanted = jnp.where(pick_in < 8, 120 + pick_in, jnp.where(jnp.logical_and(pick_in >= 16, pick_in < 24), pick_in - 16, -1))
    picks = jnp.logical_and(pick_row // LANES == pick_lane // 32, pick_col == wanted).astype(F32).astype(BF16)

    for side in range(2):
        settle(recv_w.at[side], w_r.at[side])
    for f, (ref, strip_ref) in enumerate(((free, strip_free), (tau_x, strip_tau_x), (tau_y, strip_tau_y))):
        gain = 1.0 / 1.5 if f == 0 else 0.5
        whole = flat_field(f)
        for row in range(ROWS):
            ref[row * 8 : row * 8 + 8, :] = jnp.broadcast_to(whole[row : row + 1] * gain, (8, LANES))
        padded[0:8, :] = jnp.zeros((8, LANES), F32)
        padded[8 + ROWS :, :] = jnp.zeros((8, LANES), F32)
        padded[8 : 8 + ROWS, :] = whole
        parts = [padded[4 + 16 * q : 4 + 16 * q + STRIP_ROWS, :].astype(BF16) for q in range(4)]
        own = dot(jnp.concatenate(parts, axis=1), picks)
        flat_halo[...] = jnp.zeros(flat_halo.shape, F32)
        for q in range(4):
            for g in range(max(0, 2 * q - 1), min(GROUPS, 2 * q + 3)):
                start = 8 + 8 * g - 16 * q + EDGE_ROWS
                flat_halo[start : start + 8, :] += strip_edges(recv_w[0], recv_w[1], f * GROUPS + g, q)
        whole = (own + flat_halo[8 : 8 + STRIP_ROWS, :]) * gain
        for row in range(STRIP_ROWS):
            strip_ref[row * 8 : row * 8 + 8, :] = jnp.broadcast_to(whole[row : row + 1], (8, LANES))

    none = jnp.zeros((8, LANES), F32)
    for ref in (field_x, field_y, normal_x, normal_y, shear):
        ref[0:8, :] = none
        ref[(ROWS + 1) * 8 :, :] = none
    for ref in (strip_x, strip_y, strip_normal_x, strip_normal_y, strip_shear):
        ref[0:8, :] = none
        ref[(STRIP_ROWS + 1) * 8 :, :] = none
    for v in range(FIELDS):
        recv_c[v, 0 : EDGE_ROWS * 8, :] = jnp.zeros((EDGE_ROWS * 8, LANES), BF16)
        recv_c[v, (EDGE_ROWS + ROWS) * 8 :, :] = jnp.zeros((EDGE_ROWS * 8, LANES), BF16)

    for g in range(GROUPS):
        settle(recv_e.at[g], e_r.at[g])
    for row in range(STRIP_ROWS):
        for v in range(FIELDS):
            total = none
            for q in range(4):
                at = 16 * q - EDGE_ROWS + row
                if 0 <= at < ROWS:
                    edges = recv_e[at // RB].astype(F32)
                    total = total + strip_edges(edges[:8], edges[8:], v * RB + at % RB, q)
            strip_halo[v, row * 8 : row * 8 + 8, :] = total

    def pressure(x):
        return 0.125 * (jnp.maximum(x, 0.0) + jnp.log1p(jnp.exp(-jnp.abs(x))))

    strip_rows = STRIP_ROWS * 8
    for v in range(FIELDS):
        for g in range(GROUPS):
            settle(recv_c.at[v, pl.ds(EDGE_ROWS * 8 + g * 64, 64)], c_r.at[v, g])
        parts = [recv_c[v, 128 * q : 128 * q + strip_rows, :] for q in range(4)]
        strip = dot(jnp.concatenate(parts, axis=1), picks) + strip_halo[v]
        main = recv_c[v, EDGE_ROWS * 8 : (EDGE_ROWS + ROWS) * 8, :].astype(F32)
        if v == 0:
            row = iota((strip_rows, LANES), 0) // 8
            group = iota((strip_rows, LANES), 1) // 32
            outside = jnp.logical_or(
                jnp.logical_and(group == 0, row < EDGE_ROWS), jnp.logical_and(group == 3, row >= STRIP_ROWS - EDGE_ROWS)
            )
            strip_press[...] = jnp.where(outside, 0.0, pressure(strip))
            press[...] = pressure(main)
            final[0] = main
        else:
            (strip_x, strip_y)[v - 1][8 : 8 + strip_rows, :] = strip
            (field_x, field_y)[v - 1][8 : 8 + ROWS * 8, :] = main

    def difference(x):
        return pltpu.roll(x, LANES - 1, 1) - pltpu.roll(x, 1, 1)

    main_refs = (field_x, field_y, normal_x, normal_y, shear, press, free, tau_x, tau_y)
    strip_refs = (
        strip_x, strip_y, strip_normal_x, strip_normal_y, strip_shear, strip_press, strip_free, strip_tau_x, strip_tau_y,
    )
    height = 64
    blocks = [(main_refs, i) for i in range(ROWS * 8 // height)]
    for i in range(strip_rows // height):
        blocks.insert(3 * i + 2, (strip_refs, i))

    for sweep in range(2):
        for refs, i in blocks:
            f_x, f_y, n_x, n_y, s_xy, p_ref = refs[:6]
            up, here, down = (slice(i * height + 8 * k, (i + 1) * height + 8 * k) for k in range(3))
            across_x, across_y = difference(f_x[here, :]), difference(f_y[here, :])
            along_x = f_x[down, :] - f_x[up, :]
            along_y = f_y[down, :] - f_y[up, :]
            p = p_ref[up, :]
            spread = across_x + along_y - 1.0
            skew = 0.25 * (across_x - along_y)
            new = (p * (spread + skew), p * (spread - skew), (0.5 * p) * (along_x + across_y))
            for ref, term in zip((n_x, n_y, s_xy), new):
                ref[here, :] = term if sweep == 0 else 0.5 * ref[here, :] + term
        for refs, i in blocks:
            f_x, f_y, n_x, n_y, s_xy, _, open_ref, t_x, t_y = refs
            up, here, down = (slice(i * height + 8 * k, (i + 1) * height + 8 * k) for k in range(3))
            force_x = difference(n_x[here, :]) + (s_xy[down, :] - s_xy[up, :])
            force_y = difference(s_xy[here, :]) + (n_y[down, :] - n_y[up, :])
            f_x[here, :] = open_ref[up, :] * (f_x[here, :] + t_x[up, :] + 0.25 * force_x)
            f_y[here, :] = open_ref[up, :] * (f_y[here, :] + t_y[up, :] + 0.25 * force_y)

    writes = [pltpu.make_async_copy(result.at[:, v], out_hbm.at[:, v], out_s.at[v]) for v in range(FIELDS)]
    for v in range(FIELDS):
        if v:
            ref, strip_ref = ((field_x, strip_x), (field_y, strip_y))[v - 1]
            for row in range(0, ROWS, 4):
                q, at = row // 16, row % 16 + EDGE_ROWS + 1
                main = ref[(row + 1) * 8 : (row + 5) * 8, :]
                edge = strip_ref[at * 8 : at * 8 + 32, :]
                col = iota((32, LANES), 1)
                main = jnp.where(col < HALO, pltpu.roll(edge, (LANES - 32 * q - 16) % LANES, 1), main)
                main = jnp.where(col >= LANES - HALO, pltpu.roll(edge, (120 - 32 * q) % LANES, 1), main)
                final[v, row * 8 : row * 8 + 32, :] = main
        for j in range(GROUPS):
            for start in range(0, ROWS, 16):
                parts = [final[v, pl.ds((start + h * 8) * 8 + j, 8, stride=8), :] for h in range(2)]
                result[j, v, start : start + 16, :] = jnp.concatenate(parts, axis=0).astype(BF16)
        writes[v].start()

    for write in writes:
        write.wait()

    for step in range(GROUPS):
        to, _ = member_device(step)
        pairs = [(thick.at[1, 0], at_s.at[step]), (drift.at[0], ad_s.at[step]), (send_e.at[to], e_s.at[step])]
        pairs += [(send_c.at[v, to], c_s.at[v, step]) for v in range(FIELDS)]
        for src, sem in pairs:
            if step == 0:
                wait_sent(at_home, src, sem)
            else:
                settle(src, sem)
    wait_sent(obs_home, send_obs, ob_s.at[0])
    wait_sent(obs_home, index, ob_s.at[1])
    for side in range(2):
        settle(send_w.at[side], w_s.at[side])
        settle(obs.at[1], b_s.at[side, 8])
        settle(edge_send.at[side], n_s.at[side])
        for j in range(GROUPS):
            settle(thick.at[1, j], b_s.at[side, j])


def body(tiles, background, obs_value, obs_var, obs_index, ice_mask, wind_stress):
    dma = pltpu.SemaphoreType.DMA
    return pl.pallas_call(
        functools.partial(kernel, tiles),
        out_shape=jax.ShapeDtypeStruct(background.shape, BF16),
        in_specs=[pl.BlockSpec(memory_space=pltpu.HBM)] * 6,
        out_specs=pl.BlockSpec(memory_space=pltpu.HBM),
        scratch_shapes=[
            pltpu.VMEM(obs_value.shape, BF16),
            pltpu.VMEM(obs_var.shape, BF16),
            pltpu.VMEM(ice_mask.shape, jnp.int32),
            pltpu.VMEM(wind_stress.shape, BF16),
            pltpu.VMEM((3, ENS * RB, LANES), F32),
            pltpu.VMEM((16, LANES), BF16),
            pltpu.VMEM((3, GROUPS, 8, RB, LANES), BF16),
            pltpu.VMEM((GROUPS, 8, 2, RB, LANES), BF16),
            pltpu.VMEM((3, 16, LANES), BF16),
            pltpu.VMEM((PATCHES, obs_index.shape[2]), jnp.int32),
            pltpu.VMEM((3, PATCHES, RB, LANES), F32),
            pltpu.VMEM((PATCHES, RB, LANES), F32),
            pltpu.VMEM((80, CELLS), BF16),
            pltpu.VMEM((80, CELLS), BF16),
            pltpu.VMEM((WIDE, CELLS), BF16),
            pltpu.VMEM((WIDE, CELLS), BF16),
            pltpu.VMEM((80, WIDE), F32),
            pltpu.VMEM((WIDE, FIELDS * RB * LANES), BF16),
            pltpu.VMEM((2, ENS, LANES), F32),
            pltpu.VMEM((2, ENS, LANES), BF16),
            pltpu.VMEM((2, ENS, LANES), BF16),
            pltpu.VMEM((FIELDS, GROUPS, 64, LANES), BF16),
            pltpu.VMEM((FIELDS, (ROWS + 2 * EDGE_ROWS) * 8, LANES), BF16),
            pltpu.VMEM((GROUPS, 16, LANES), BF16),
            pltpu.VMEM((GROUPS, 16, LANES), BF16),
            pltpu.VMEM((2, RB, LANES), F32),
            pltpu.VMEM((2, RB, LANES), F32),
            pltpu.VMEM((ROWS + 16, LANES), F32),
            pltpu.VMEM((STRIP_ROWS + 16, LANES), F32),
            pltpu.VMEM((FIELDS, STRIP_ROWS * 8, LANES), F32),
            *[pltpu.VMEM((ROWS * 8, LANES), F32)] * 4,
            *[pltpu.VMEM(((ROWS + 2) * 8, LANES), F32)] * 5,
            *[pltpu.VMEM((STRIP_ROWS * 8, LANES), F32)] * 4,
            *[pltpu.VMEM(((STRIP_ROWS + 2) * 8, LANES), F32)] * 5,
            pltpu.VMEM((FIELDS, ROWS * 8, LANES), F32),
            pltpu.VMEM(background.shape, BF16),
            dma((4,)),
            dma((FIELDS,)),
            dma((GROUPS,)), dma((GROUPS,)),
            dma((GROUPS,)), dma((GROUPS,)),
            dma((2,)), dma((2,)),
            dma((2, 9)), dma((3, 9)),
            dma((2,)), dma((2,)),
            dma((FIELDS, GROUPS)), dma((FIELDS, GROUPS)),
            dma((GROUPS,)), dma((GROUPS,)),
            dma((2,)), dma((2,)),
        ],
        compiler_params=pltpu.CompilerParams(
            collective_id=0, has_side_effects=True, vmem_limit_bytes=60 * 1024 * 1024
        ),
        name="analysis_and_drift",
    )(background.reshape(8, FIELDS, GROUPS, RB, LANES), obs_value, obs_var, obs_index[0], ice_mask, wind_stress)


def solution(mesh):
    placed = (
        P("mem", None, None, "tile"),
        P("mem", "tile"),
        P("mem", "tile"),
        P("mem", "tile", None),
        P(None, "tile"),
        P(None, None, "tile"),
    )
    return jax.shard_map(
        functools.partial(body, mesh.shape["tile"]),
        mesh=mesh,
        in_specs=placed,
        out_specs=P("mem", None, None, "tile"),
        check_vma=False,
    )
```

```python
import functools

import jax
import jax.numpy as jnp
from jax import lax
from jax.experimental import pallas as pl
from jax.experimental.pallas import tpu as pltpu
from jax.sharding import PartitionSpec as P

F32 = jnp.float32
BF16 = jnp.bfloat16
MESH = pl.DeviceIdType.MESH

ENS = 64
GROUPS = 8
RB = 8
ROWS = 64
PC = 16
W = 128
SPAN = PC + 2 * W
LANES = 128
PATCHES = 8
FIELDS = 3
NS_ITERS = 6
WIDE = PATCHES * ENS
CELLS = 3 * RB * LANES
HALO = 4
EDGE_ROWS = 4
STRIP_ROWS = 16 + 2 * EDGE_ROWS


def iota(shape, axis):
    return lax.broadcasted_iota(jnp.int32, shape, axis)


def aligned(start, size, by):
    return pl.ds(pl.multiple_of(start, by), size)


def split(x):
    high = x.astype(BF16)
    return high, (x - high.astype(F32)).astype(BF16)


def dot(a, b):
    return jnp.dot(a, b, preferred_element_type=F32)


def dot_lanes(a, b):
    return lax.dot_general(a, b, (((1,), (1,)), ((), ())), preferred_element_type=F32)


def block_diagonal(x):
    segment = iota(x.shape, 1) // ENS
    zero = jnp.zeros_like(x)
    return jnp.concatenate([jnp.where(segment == q, x, zero) for q in range(4)], axis=0)


def patch_products(left, right, left_parts=2, right_parts=2):
    rows = left.shape[0]
    left_high, left_low = split(left)
    right_high, right_low = split(right)
    out = []
    for half in range(2):
        lanes = slice(half * 256, (half + 1) * 256)
        main = block_diagonal(right_high[:, lanes])
        if left_parts == 2:
            both = dot(jnp.concatenate([left_high[:, lanes], left_low[:, lanes]], axis=0), main)
            total = both[:rows] + both[rows:]
        else:
            total = dot(left_high[:, lanes], main)
        if right_parts == 2:
            total = total + dot(left_high[:, lanes], block_diagonal(right_low[:, lanes]))
        out.append(total)
    return jnp.concatenate(out, axis=1)


def root_weights(system, projected):
    row = iota((ENS, WIDE), 0)
    eye = ((iota((ENS, WIDE), 1) % ENS) == row).astype(F32)
    full = system + (ENS - 1.0) * eye
    squares = jnp.sum(full * full, axis=0, keepdims=True)
    own = ((iota((PATCHES, WIDE), 1) // ENS) == iota((PATCHES, WIDE), 0)).astype(F32)
    norm = jnp.sum(own * squares, axis=1, keepdims=True)
    scale = jnp.sqrt(jnp.sum(own * norm, axis=0, keepdims=True))
    centring = eye - 1.0 / ENS
    iterate = (system + (ENS - 1.0) * centring) / scale
    inverse_root = centring
    for sweep in range(NS_ITERS):
        last = sweep == NS_ITERS - 1
        parts = 2 if last else 1
        product = patch_products(inverse_root, iterate, parts, parts) if sweep else iterate
        change = 0.5 * (eye - product)
        held = jnp.concatenate(([] if last else [iterate]) + [inverse_root, projected], axis=0)
        held = held + patch_products(held, change, 2, parts)
        if not last:
            iterate, held = held[:ENS], held[ENS:]
        inverse_root, projected = held[:ENS], held[ENS:]
    mean_weight = patch_products(projected, inverse_root)[:1] / scale
    return jnp.sqrt(ENS - 1.0) * (inverse_root / jnp.sqrt(scale)) + (mean_weight + 1.0 / ENS)


def kernel(
    tiles,
    prior, obs_value_hbm, obs_var_hbm, obs_index, mask_hbm, wind_hbm,
    out,
    obs_value, obs_var, ice_mask, wind,
    staged, tall, send_obs, thick, drift, obs, index,
    count, weight, anom_hi, anom_lo, pulls, heavy, acc, projected,
    masked, packed, edge_send, edge_recv,
    send_c, recv_c, send_e, recv_e,
    flat_rows, send_w, recv_w, padded, flat_halo, strip_halo,
    free, tau_x, tau_y, press, field_x, field_y, normal_x, normal_y, shear,
    strip_free, strip_tau_x, strip_tau_y, strip_press, strip_x, strip_y, strip_normal_x, strip_normal_y, strip_shear,
    final,
    in_s, at_s, at_r, ad_s, ad_r, ob_s, ob_r, b_s, b_r, n_s, n_r, c_s, c_r, e_s, e_r, w_s, w_r,
):
    me, tile = lax.axis_index("mem"), lax.axis_index("tile")
    core, z_lo = me % 2, me // 2
    half, ring = tile % 2, tile // 2
    z = half * 4 + z_lo

    def ring_device(at_z, at_core):
        return ((at_z % 4) * 2 + at_core, ring * 2 + at_z // 4)

    chip_mate = (me + 1 - 2 * core, tile)
    side_mate = (me + 1 - 2 * core, lax.rem(tile + tiles - 2 + 4 * core, tiles))

    loads = [
        pltpu.make_async_copy(src, dst, in_s.at[i])
        for i, (src, dst) in enumerate(
            (
                (prior.at[:, 0], staged.at[:, 0]),
                (obs_value_hbm, obs_value),
                (obs_var_hbm, obs_var),
                (mask_hbm, ice_mask),
                (wind_hbm, wind),
                (prior.at[:, pl.ds(1, 2)], staged.at[:, pl.ds(1, 2)]),
            )
        )
    ]
    for load in loads:
        load.start()

    barrier = pltpu.get_barrier_semaphore()

    def greet(step, carry):
        at = lax.rem(z * 2 + core + lax.rem(step + 7, 15) + 1, 16)
        pl.semaphore_signal(barrier, inc=1, device_id=ring_device(at // 2, at % 2), device_id_type=MESH)
        return carry

    lax.fori_loop(1, 16, greet, 0)
    pl.semaphore_signal(barrier, inc=1, device_id=side_mate, device_id_type=MESH)

    for load in loads:
        load.wait()
    flat_rows[0] = ice_mask[...].astype(F32)
    flat_rows[1] = wind[0].astype(F32)
    flat_rows[2] = wind[1].astype(F32)
    rows = pl.ds(pl.multiple_of(me * RB, RB), RB)
    surface = [obs_value[...].astype(F32), obs_var[...].astype(F32)]
    surface += [flat_rows[f, rows, :] for f in range(FIELDS)]
    send_obs[...] = jnp.concatenate(surface + [jnp.zeros((RB, LANES), F32)], axis=0).astype(BF16)

    pl.semaphore_wait(barrier, 16)

    def remote(src, dst, s_sem, r_sem, device):
        return pltpu.make_async_remote_copy(
            src_ref=src, dst_ref=dst, send_sem=s_sem, recv_sem=r_sem, device_id=device, device_id_type=MESH
        )

    def settle(ref, sem):
        pltpu.make_async_copy(ref, ref, sem).wait()

    def send_or_keep(same, src, dst, s_sem, r_sem, device):
        @pl.when(same)
        def _():
            pltpu.make_async_copy(src, dst, r_sem).start()

        @pl.when(jnp.logical_not(same))
        def _():
            remote(src, dst, s_sem, r_sem, device).start()

    def wait_sent(same, src, s_sem):
        @pl.when(jnp.logical_not(same))
        def _():
            settle(src, s_sem)

    owner = ring_device(me, half)
    obs_home = jnp.logical_and(owner[0] == me, owner[1] == tile)
    send_or_keep(obs_home, obs_index, index, ob_s.at[1], ob_r.at[1], owner)
    at_home = core == half
    far_first = (4, 3, 5, 2, 6, 1, 7, 0)
    for step in far_first:
        g = lax.rem(z + step, GROUPS)
        there = ring_device(g, half)
        if step:
            remote(staged.at[:, 0, g], thick.at[1, me], at_s.at[0], at_r.at[me], there).start()
        else:
            send_or_keep(at_home, staged.at[:, 0, g], thick.at[1, me], at_s.at[0], at_r.at[me], there)
    send_or_keep(obs_home, send_obs, obs.at[1], ob_s.at[0], ob_r.at[0], owner)
    mate_slot = 2 * core
    side_slot = 2 - 2 * core
    chips = (z_lo, z_lo + 1 - 2 * (z_lo % 2), z_lo + 2 - 4 * (z_lo // 2), 3 - z_lo)
    apart = (core + half) % 2

    def pass_on(i):
        chip = chips[i] * (1 - apart) + chips[3 - i] * apart
        for c in range(2):
            j = chip * 2 + c
            settle(thick.at[1, j], at_r.at[j])
            remote(thick.at[1, j], thick.at[side_slot, j], b_s.at[0], b_r.at[side_slot, 0], side_mate).start()
            remote(thick.at[1, j], thick.at[mate_slot, j], b_s.at[0], b_r.at[mate_slot, 0], chip_mate).start()

    for i in range(3):
        pass_on(i)

    settle(index, ob_r.at[1])
    cell = index[...].astype(F32)
    cell_row = jnp.floor((cell + 0.5) * (1.0 / SPAN))
    cell_col = cell - SPAN * cell_row
    row_at = iota((16, cell.shape[1]), 0).astype(F32)
    col_at = iota((3 * LANES, cell.shape[1]), 0).astype(F32)
    for p in range(PATCHES):
        rows = (row_at == cell_row[p : p + 1]).astype(F32).astype(BF16)
        cols = (col_at == cell_col[p : p + 1] + float(p * PC)).astype(F32).astype(BF16)
        hits = dot_lanes(rows, cols)
        for s in range(3):
            count[s, p] = hits[:RB, s * LANES : (s + 1) * LANES]

    settle(obs.at[1], ob_r.at[0])
    remote(obs.at[1], obs.at[side_slot], b_s.at[1], b_r.at[side_slot, 1], side_mate).start()
    remote(obs.at[1], obs.at[mate_slot], b_s.at[1], b_r.at[mate_slot, 1], chip_mate).start()
    pass_on(3)
    for step in far_first:
        g = lax.rem(z + step, GROUPS)
        there = ring_device(g, half)
        if step:
            remote(staged.at[:, pl.ds(1, 2), g], drift.at[me], ad_s.at[0], ad_r.at[0], there).start()
        else:
            send_or_keep(at_home, staged.at[:, pl.ds(1, 2), g], drift.at[me], ad_s.at[0], ad_r.at[0], there)

    def system_part(s, place):
        both = obs[s].astype(F32)
        values, variance = both[:RB], both[RB : 2 * RB]
        for p in range(PATCHES):
            weight[p * RB : (p + 1) * RB, :] = count[s, p] / variance
        tall[place] = thick[s].astype(F32).reshape(ENS * RB, LANES)

        def rows_pair(pair, carry):
            for h in range(2):
                r = pair * 2 + h
                x = tall[place, pl.ds(r, ENS, stride=RB), :]
                mean = jnp.sum(x, axis=0, keepdims=True) * (1.0 / ENS)
                anom = x - mean
                value = jnp.sum(jnp.where(iota((RB, LANES), 0) == r, values, 0.0), axis=0, keepdims=True)
                lanes = aligned((place * RB + r) * LANES, LANES, LANES)
                anom_hi[:, lanes], anom_lo[:, lanes] = split(anom)
                pull = weight[pl.ds(r, PATCHES, stride=RB), :] * (value - mean)
                pull_high = pull.astype(BF16).astype(F32)
                pulls[:, lanes] = jnp.concatenate([pull_high, pull - pull_high], axis=0).astype(BF16)
                for p in range(PATCHES):
                    heavy[p * ENS : (p + 1) * ENS, lanes] = (anom * weight[pl.ds(p * RB + r, 1), :]).astype(BF16)
            return carry

        lax.fori_loop(0, RB // 2, rows_pair, 0)
        span = slice(place * RB * LANES, (place + 1) * RB * LANES)
        main = dot_lanes(jnp.concatenate([anom_hi[:, span], anom_lo[:, span]], axis=0), heavy[:, span])
        part = main[:ENS] + main[ENS:]
        drawn = dot_lanes(pulls[:, span], anom_hi[:, span]) + dot_lanes(pulls[:, span], anom_lo[:, span])
        drawn = drawn[:PATCHES] + drawn[PATCHES:]
        if place == 0:
            acc[...] = part
            projected[...] = drawn
        else:
            acc[...] += part
            projected[...] += drawn

    system_part(1, 0)

    edge_lane = iota((ENS, LANES), 1)

    def spread(v):
        for r in range(RB):
            j = v * RB + r
            x = tall[v, pl.ds(r, ENS, stride=RB), :]
            here = (edge_lane // HALO) == j
            low = pltpu.roll(x, (HALO * j) % LANES, 1)
            high = pltpu.roll(x, (HALO * j + HALO) % LANES, 1)
            if j == 0:
                packed[0] = jnp.where(here, low, 0.0)
                packed[1] = jnp.where(here, high, 0.0)
            else:
                packed[0] = jnp.where(here, low, packed[0])
                packed[1] = jnp.where(here, high, packed[1])
            for p in range(PATCHES):
                masked[p * ENS : (p + 1) * ENS, j * LANES : (j + 1) * LANES] = jnp.where(
                    edge_lane // PC == p, x, 0.0
                ).astype(BF16)

    spread(0)

    def member_device(step):
        to = lax.rem(me + step, GROUPS)
        return to, (to, ring * 2 + core)

    for place, s in ((1, 2 - 2 * core), (2, 2 * core)):
        settle(obs.at[s], b_r.at[s, 1])
        if place == 2:
            sides = []
            for side, first in ((0, LANES - HALO), (2, 0)):
                surface = obs[side].astype(F32)
                total = jnp.zeros((RB, LANES), F32)
                for f in range(FIELDS):
                    at = (f * GROUPS + z) * HALO
                    moved = pltpu.roll(surface[(f + 2) * RB : (f + 3) * RB], lax.rem(at - first + LANES, LANES), 1)
                    spot = iota((RB, LANES), 1) // HALO == f * GROUPS + z
                    total = jnp.where(spot, moved, total)
                sides.append(total)
            send_w[...] = jnp.concatenate(sides, axis=0).astype(BF16)
            for step in far_first:
                to, there = member_device(step)
                if step:
                    remote(send_w, recv_w.at[z], w_s.at[0], w_r.at[0], there).start()
                else:
                    send_or_keep(at_home, send_w, recv_w.at[z], w_s.at[0], w_r.at[0], there)
        settle(thick.at[s], b_r.at[s, 0])
        system_part(s, place)

    own_lanes = iota((PATCHES, WIDE), 1) // ENS == iota((PATCHES, WIDE), 0)
    drawn = jnp.where(own_lanes, jnp.concatenate([projected[...]] * PATCHES, axis=1), 0.0)
    drawn = jnp.broadcast_to(jnp.sum(drawn, axis=0, keepdims=True), (16, WIDE))
    weights = root_weights(acc[...], drawn)
    left = jnp.concatenate(split(weights), axis=0)

    for v in range(FIELDS):
        if v == 1:
            settle(drift, ad_r.at[0])
            for f in (1, 2):
                tall[f] = drift[:, :, f - 1].astype(F32).reshape(ENS * RB, LANES)
                spread(f)
            for side, p in ((0, 0), (1, PATCHES - 1)):
                edge = dot(left[:, p * ENS : (p + 1) * ENS], packed[side].astype(BF16))
                edge_send[side] = (edge[:ENS] + edge[ENS:]).astype(BF16)
            remote(edge_send.at[1 - core], edge_recv.at[core], n_s.at[0], n_r.at[0], chip_mate).start()
            remote(edge_send.at[core], edge_recv.at[1 - core], n_s.at[0], n_r.at[0], side_mate).start()
        for pair in range(RB // 2):
            at = (v * RB + pair * 2) * LANES
            got = dot(left, masked[:, at : at + 256])
            got = got[:ENS] + got[ENS:]
            for to in range(GROUPS):
                rows = slice(to * 8, to * 8 + 8)
                send_c[v, to, pair * 16 : pair * 16 + 16, :] = jnp.concatenate(
                    [got[rows, :LANES], got[rows, LANES:]], axis=0
                ).astype(BF16)
        for step in far_first:
            to, there = member_device(step)
            if step:
                remote(send_c.at[v, to], recv_c.at[v, aligned(EDGE_ROWS * 8 + z * 64, 64, 16)], c_s.at[0], c_r.at[v], there).start()
            else:
                send_or_keep(at_home, send_c.at[v, to], recv_c.at[v, aligned(EDGE_ROWS * 8 + z * 64, 64, 16)], c_s.at[0], c_r.at[v], there)
    at_lane = iota((8, LANES), 1)
    lane_group, lane_in = at_lane // 32, at_lane % 32
    is_right = jnp.logical_and(lane_in >= 8, lane_in < 12)
    is_left = jnp.logical_and(lane_in >= 12, lane_in < 16)

    def strip_edges(from_left, from_right, j, q):
        left_part = pltpu.roll(from_left, (32 * q + 12 - HALO * j) % LANES, 1)
        right_part = pltpu.roll(from_right, (32 * q + 8 - HALO * j) % LANES, 1)
        here = lane_group == q
        part = jnp.where(jnp.logical_and(here, is_left), left_part, 0.0)
        return jnp.where(jnp.logical_and(here, is_right), right_part, part)

    pick_row, pick_lane = iota((4 * LANES, LANES), 0), iota((4 * LANES, LANES), 1)
    pick_col, pick_in = pick_row % LANES, pick_lane % 32
    wanted = jnp.where(pick_in < 8, 120 + pick_in, jnp.where(jnp.logical_and(pick_in >= 16, pick_in < 24), pick_in - 16, -1))
    picks = jnp.logical_and(pick_row // LANES == pick_lane // 32, pick_col == wanted).astype(F32).astype(BF16)

    none = jnp.zeros((8, LANES), F32)
    for ref in (field_x, field_y, normal_x, normal_y, shear):
        ref[0:8, :] = none
        ref[(ROWS + 1) * 8 :, :] = none
    for ref in (strip_x, strip_y, strip_normal_x, strip_normal_y, strip_shear):
        ref[0:8, :] = none
        ref[(STRIP_ROWS + 1) * 8 :, :] = none
    for v in range(FIELDS):
        recv_c[v, 0 : EDGE_ROWS * 8, :] = jnp.zeros((EDGE_ROWS * 8, LANES), BF16)
        recv_c[v, (EDGE_ROWS + ROWS) * 8 :, :] = jnp.zeros((EDGE_ROWS * 8, LANES), BF16)

    settle(edge_recv, n_r.at[0])
    for to in range(GROUPS):
        rows = slice(to * 8, to * 8 + 8)
        send_e[to] = jnp.concatenate(
            [edge_recv[0].astype(F32)[rows], edge_recv[1].astype(F32)[rows]], axis=0
        ).astype(BF16)
    for step in far_first:
        to, there = member_device(step)
        if step:
            remote(send_e.at[to], recv_e.at[z], e_s.at[0], e_r.at[0], there).start()
        else:
            send_or_keep(at_home, send_e.at[to], recv_e.at[z], e_s.at[0], e_r.at[0], there)

    settle(recv_w, w_r.at[0])
    edges = jnp.sum(recv_w[...].astype(F32), axis=0)
    for f, (ref, strip_ref) in enumerate(((free, strip_free), (tau_x, strip_tau_x), (tau_y, strip_tau_y))):
        gain = 1.0 / 1.5 if f == 0 else 0.5
        whole = flat_rows[f]
        for row in range(ROWS):
            ref[row * 8 : row * 8 + 8, :] = jnp.broadcast_to(whole[row : row + 1] * gain, (8, LANES))
        padded[0:8, :] = jnp.zeros((8, LANES), F32)
        padded[8 + ROWS :, :] = jnp.zeros((8, LANES), F32)
        padded[8 : 8 + ROWS, :] = whole
        parts = [padded[4 + 16 * q : 4 + 16 * q + STRIP_ROWS, :].astype(BF16) for q in range(4)]
        own = dot(jnp.concatenate(parts, axis=1), picks)
        flat_halo[...] = jnp.zeros(flat_halo.shape, F32)
        for q in range(4):
            for g in range(max(0, 2 * q - 1), min(GROUPS, 2 * q + 3)):
                start = 8 + 8 * g - 16 * q + EDGE_ROWS
                flat_halo[start : start + 8, :] += strip_edges(edges[:RB], edges[RB:], f * GROUPS + g, q)
        whole = (own + flat_halo[8 : 8 + STRIP_ROWS, :]) * gain
        for row in range(STRIP_ROWS):
            strip_ref[row * 8 : row * 8 + 8, :] = jnp.broadcast_to(whole[row : row + 1], (8, LANES))

    def pressure(x):
        return 0.125 * (jnp.maximum(x, 0.0) + jnp.log1p(jnp.exp(-jnp.abs(x))))

    def unpack(v):
        settle(recv_c.at[v, pl.ds(EDGE_ROWS * 8, ROWS * 8)], c_r.at[v])
        main = recv_c[v, EDGE_ROWS * 8 : (EDGE_ROWS + ROWS) * 8, :].astype(F32)
        if v == 0:
            press[...] = pressure(main)
            final[0] = main
        else:
            (field_x, field_y)[v - 1][8 : 8 + ROWS * 8, :] = main

    def write_out(v):
        for j in range(GROUPS):
            for start in range(0, ROWS, 16):
                parts = [final[v, pl.ds((start + h * 8) * 8 + j, 8, stride=8), :] for h in range(2)]
                out[j, v, start : start + 16, :] = jnp.concatenate(parts, axis=0).astype(BF16)

    unpack(0)
    write_out(0)
    unpack(1)
    settle(recv_e, e_r.at[0])
    for row in range(STRIP_ROWS):
        for v in range(FIELDS):
            total = none
            for q in range(4):
                at = 16 * q - EDGE_ROWS + row
                if 0 <= at < ROWS:
                    edges = recv_e[at // RB].astype(F32)
                    total = total + strip_edges(edges[:8], edges[8:], v * RB + at % RB, q)
            strip_halo[v, row * 8 : row * 8 + 8, :] = total
    unpack(2)

    strip_rows = STRIP_ROWS * 8
    for v in range(FIELDS):
        parts = [recv_c[v, 128 * q : 128 * q + strip_rows, :] for q in range(4)]
        strip = dot(jnp.concatenate(parts, axis=1), picks) + strip_halo[v]
        if v == 0:
            row = iota((strip_rows, LANES), 0) // 8
            group = iota((strip_rows, LANES), 1) // 32
            outside = jnp.logical_or(
                jnp.logical_and(group == 0, row < EDGE_ROWS), jnp.logical_and(group == 3, row >= STRIP_ROWS - EDGE_ROWS)
            )
            strip_press[...] = jnp.where(outside, 0.0, pressure(strip))
        else:
            (strip_x, strip_y)[v - 1][8 : 8 + strip_rows, :] = strip

    def difference(x):
        return pltpu.roll(x, LANES - 1, 1) - pltpu.roll(x, 1, 1)

    main_refs = (field_x, field_y, normal_x, normal_y, shear, press, free, tau_x, tau_y)
    strip_refs = (
        strip_x, strip_y, strip_normal_x, strip_normal_y, strip_shear, strip_press, strip_free, strip_tau_x, strip_tau_y,
    )
    height = 64
    blocks = [(main_refs, i) for i in range(ROWS * 8 // height)]
    for i in range(strip_rows // height):
        blocks.insert(3 * i + 2, (strip_refs, i))

    for sweep in range(2):
        for refs, i in blocks:
            f_x, f_y, n_x, n_y, s_xy, p_ref = refs[:6]
            up, here, down = (slice(i * height + 8 * k, (i + 1) * height + 8 * k) for k in range(3))
            across_x, across_y = difference(f_x[here, :]), difference(f_y[here, :])
            along_x = f_x[down, :] - f_x[up, :]
            along_y = f_y[down, :] - f_y[up, :]
            p = p_ref[up, :]
            spread = across_x + along_y - 1.0
            skew = 0.25 * (across_x - along_y)
            new = (p * (spread + skew), p * (spread - skew), (0.5 * p) * (along_x + across_y))
            for ref, term in zip((n_x, n_y, s_xy), new):
                ref[here, :] = term if sweep == 0 else 0.5 * ref[here, :] + term
        for refs, i in blocks:
            f_x, f_y, n_x, n_y, s_xy, _, open_ref, t_x, t_y = refs
            up, here, down = (slice(i * height + 8 * k, (i + 1) * height + 8 * k) for k in range(3))
            force_x = difference(n_x[here, :]) + (s_xy[down, :] - s_xy[up, :])
            force_y = difference(s_xy[here, :]) + (n_y[down, :] - n_y[up, :])
            f_x[here, :] = open_ref[up, :] * (f_x[here, :] + t_x[up, :] + 0.25 * force_x)
            f_y[here, :] = open_ref[up, :] * (f_y[here, :] + t_y[up, :] + 0.25 * force_y)

    for v, (ref, strip_ref) in ((1, (field_x, strip_x)), (2, (field_y, strip_y))):
        for row in range(0, ROWS, 4):
            q, at = row // 16, row % 16 + EDGE_ROWS + 1
            main = ref[(row + 1) * 8 : (row + 5) * 8, :]
            edge = strip_ref[at * 8 : at * 8 + 32, :]
            col = iota((32, LANES), 1)
            main = jnp.where(col < HALO, pltpu.roll(edge, (LANES - 32 * q - 16) % LANES, 1), main)
            main = jnp.where(col >= LANES - HALO, pltpu.roll(edge, (120 - 32 * q) % LANES, 1), main)
            final[v, row * 8 : row * 8 + 32, :] = main
        write_out(v)

    settle(thick.at[pl.ds(0, 2)], b_s.at[0])
    settle(obs.at[pl.ds(0, 2)], b_s.at[1])
    settle(edge_send, n_s.at[0])
    for sent, sem in ((thick.at[1], at_s), (drift, ad_s), (recv_e, e_s), (recv_w, w_s)):

        @pl.when(at_home)
        def _():
            settle(sent.at[pl.ds(0, GROUPS - 1)], sem.at[0])

        @pl.when(jnp.logical_not(at_home))
        def _():
            settle(sent, sem.at[0])

    @pl.when(at_home)
    def _():
        settle(send_c.at[:, pl.ds(0, GROUPS - 1)], c_s.at[0])

    @pl.when(jnp.logical_not(at_home))
    def _():
        settle(send_c, c_s.at[0])

    wait_sent(obs_home, send_obs, ob_s.at[0])
    wait_sent(obs_home, index, ob_s.at[1])


def body(tiles, background, obs_value, obs_var, obs_index, ice_mask, wind_stress):
    dma = pltpu.SemaphoreType.DMA
    inputs = (background.reshape(8, FIELDS, GROUPS, RB, LANES), obs_value, obs_var, obs_index[0], ice_mask, wind_stress)
    return pl.pallas_call(
        functools.partial(kernel, tiles),
        out_shape=jax.ShapeDtypeStruct(background.shape, BF16),
        in_specs=[pl.BlockSpec(memory_space=pltpu.HBM)] * 6,
        out_specs=pl.BlockSpec(memory_space=pltpu.VMEM),
        scratch_shapes=[
            pltpu.VMEM(obs_value.shape, BF16),
            pltpu.VMEM(obs_var.shape, BF16),
            pltpu.VMEM(ice_mask.shape, jnp.int32),
            pltpu.VMEM(wind_stress.shape, BF16),
            pltpu.VMEM((8, FIELDS, GROUPS, RB, LANES), BF16),
            pltpu.VMEM((3, ENS * RB, LANES), F32),
            pltpu.VMEM((48, LANES), BF16),
            pltpu.VMEM((3, GROUPS, 8, RB, LANES), BF16),
            pltpu.VMEM((GROUPS, 8, 2, RB, LANES), BF16),
            pltpu.VMEM((3, 48, LANES), BF16),
            pltpu.VMEM((PATCHES, obs_index.shape[2]), jnp.int32),
            pltpu.VMEM((3, PATCHES, RB, LANES), F32),
            pltpu.VMEM((PATCHES * RB, LANES), F32),
            pltpu.VMEM((ENS, CELLS), BF16),
            pltpu.VMEM((ENS, CELLS), BF16),
            pltpu.VMEM((16, CELLS), BF16),
            pltpu.VMEM((WIDE, CELLS), BF16),
            pltpu.VMEM((ENS, WIDE), F32),
            pltpu.VMEM((PATCHES, ENS), F32),
            pltpu.VMEM((WIDE, FIELDS * RB * LANES), BF16),
            pltpu.VMEM((2, ENS, LANES), F32),
            pltpu.VMEM((2, ENS, LANES), BF16),
            pltpu.VMEM((2, ENS, LANES), BF16),
            pltpu.VMEM((FIELDS, GROUPS, 64, LANES), BF16),
            pltpu.VMEM((FIELDS, (ROWS + 2 * EDGE_ROWS) * 8, LANES), BF16),
            pltpu.VMEM((GROUPS, 16, LANES), BF16),
            pltpu.VMEM((GROUPS, 16, LANES), BF16),
            pltpu.VMEM((FIELDS, ROWS, LANES), F32),
            pltpu.VMEM((16, LANES), BF16),
            pltpu.VMEM((GROUPS, 16, LANES), BF16),
            pltpu.VMEM((ROWS + 16, LANES), F32),
            pltpu.VMEM((STRIP_ROWS + 16, LANES), F32),
            pltpu.VMEM((FIELDS, STRIP_ROWS * 8, LANES), F32),
            *[pltpu.VMEM((ROWS * 8, LANES), F32)] * 4,
            *[pltpu.VMEM(((ROWS + 2) * 8, LANES), F32)] * 5,
            *[pltpu.VMEM((STRIP_ROWS * 8, LANES), F32)] * 4,
            *[pltpu.VMEM(((STRIP_ROWS + 2) * 8, LANES), F32)] * 5,
            pltpu.VMEM((FIELDS, ROWS * 8, LANES), F32),
            dma((6,)),
            dma((1,)), dma((GROUPS,)),
            dma((1,)), dma((1,)),
            dma((2,)), dma((2,)),
            dma((2,)), dma((3, 2)),
            dma((1,)), dma((1,)),
            dma((1,)), dma((FIELDS,)),
            dma((1,)), dma((1,)),
            dma((1,)), dma((1,)),
        ],
        compiler_params=pltpu.CompilerParams(
            collective_id=0, has_side_effects=True, vmem_limit_bytes=50 * 1024 * 1024
        ),
        name="analysis_and_drift",
    )(*[pltpu.with_memory_space_constraint(x, pltpu.HBM) for x in inputs])


def solution(mesh):
    placed = (
        P("mem", None, None, "tile"),
        P("mem", "tile"),
        P("mem", "tile"),
        P("mem", "tile", None),
        P(None, "tile"),
        P(None, None, "tile"),
    )
    return jax.shard_map(
        functools.partial(body, mesh.shape["tile"]),
        mesh=mesh,
        in_specs=placed,
        out_specs=P("mem", None, None, "tile"),
        check_vma=False,
    )
```

```python
import functools

import jax
import jax.numpy as jnp
from jax import lax
from jax.experimental import pallas as pl
from jax.experimental.pallas import tpu as pltpu
from jax.sharding import PartitionSpec as P

F32 = jnp.float32
BF16 = jnp.bfloat16
MESH = pl.DeviceIdType.MESH

ENS = 64
GROUPS = 8
RB = 8
ROWS = 64
PC = 16
W = 128
SPAN = PC + 2 * W
LANES = 128
PATCHES = 8
FIELDS = 3
NS_ITERS = 6
WIDE = PATCHES * ENS
CELLS = 3 * RB * LANES
HALO = 4
EDGE_ROWS = 4
STRIP_ROWS = 16 + 2 * EDGE_ROWS


def iota(shape, axis):
    return lax.broadcasted_iota(jnp.int32, shape, axis)


def aligned(start, size, by):
    return pl.ds(pl.multiple_of(start, by), size)


def split(x):
    high = x.astype(BF16)
    return high, (x - high.astype(F32)).astype(BF16)


def dot(a, b):
    return jnp.dot(a, b, preferred_element_type=F32)


def dot_lanes(a, b):
    return lax.dot_general(a, b, (((1,), (1,)), ((), ())), preferred_element_type=F32)


def block_diagonal(x):
    segment = iota(x.shape, 1) // ENS
    zero = jnp.zeros_like(x)
    return jnp.concatenate([jnp.where(segment == q, x, zero) for q in range(4)], axis=0)


def patch_blocks(right, parts):
    lanes = [slice(half * 256, (half + 1) * 256) for half in range(2)]
    return [[block_diagonal(part[:, at]) for part in split(right)[:parts]] for at in lanes]


def patch_products(left, blocks):
    rows = left.shape[0]
    left_high, left_low = split(left)
    out = []
    for half, parts in enumerate(blocks):
        lanes = slice(half * 256, (half + 1) * 256)
        both = dot(jnp.concatenate([left_high[:, lanes], left_low[:, lanes]], axis=0), parts[0])
        total = both[:rows] + both[rows:]
        if len(parts) == 2:
            total = total + dot(left_high[:, lanes], parts[1])
        out.append(total)
    return jnp.concatenate(out, axis=1)


def root_weights(system, projected):
    row = iota((ENS, WIDE), 0)
    eye = ((iota((ENS, WIDE), 1) % ENS) == row).astype(F32)
    full = system + (ENS - 1.0) * eye
    squares = jnp.sum(full * full, axis=0, keepdims=True)
    own = ((iota((PATCHES, WIDE), 1) // ENS) == iota((PATCHES, WIDE), 0)).astype(F32)
    norm = jnp.sum(own * squares, axis=1, keepdims=True)
    scale = jnp.sqrt(jnp.sum(own * norm, axis=0, keepdims=True))
    centring = eye - 1.0 / ENS
    product = (system + (ENS - 1.0) * centring) / scale
    inverse_root = centring
    for sweep in range(NS_ITERS):
        last = sweep == NS_ITERS - 1
        blocks = patch_blocks(0.5 * (eye - product), 2 if last else 1)
        held = jnp.concatenate(([] if last else [product]) + [inverse_root, projected], axis=0)
        held = held + patch_products(held, blocks)
        if not last:
            product, held = held[:ENS], held[ENS:]
            product = product + patch_products(product, blocks)
        inverse_root, projected = held[:ENS], held[ENS:]
    mean_weight = patch_products(projected, patch_blocks(inverse_root, 2))[:1] / scale
    return jnp.sqrt(ENS - 1.0) * (inverse_root / jnp.sqrt(scale)) + (mean_weight + 1.0 / ENS)


def kernel(
    tiles,
    prior, obs_value_hbm, obs_var_hbm, obs_index, mask_hbm, wind_hbm,
    out,
    obs_value, obs_var, ice_mask, wind,
    staged, tall, send_obs, thick, drift, obs, index,
    count, weight, anom_hi, anom_lo, pulls, heavy, heavy_lo, acc, projected,
    masked, packed, edge_send, edge_recv,
    send_c, recv_c, send_e, recv_e,
    flat_rows, padded, flat_own, flat_halo, strip_halo,
    free, tau_x, tau_y, press, field_x, field_y, normal_x, normal_y, shear,
    strip_free, strip_tau_x, strip_tau_y, strip_press, strip_x, strip_y, strip_normal_x, strip_normal_y, strip_shear,
    final,
    in_s, at_s, at_r, ad_s, ad_r, ob_s, ob_r, b_s, b_r, n_s, n_r, c_s, c_r, e_s, e_r,
):
    me, tile = lax.axis_index("mem"), lax.axis_index("tile")
    core, z_lo = me % 2, me // 2
    half, ring = tile % 2, tile // 2
    z = half * 4 + z_lo

    def ring_device(at_z, at_core):
        return ((at_z % 4) * 2 + at_core, ring * 2 + at_z // 4)

    chip_mate = (me + 1 - 2 * core, tile)
    side_mate = (me + 1 - 2 * core, lax.rem(tile + tiles - 2 + 4 * core, tiles))

    loads = [
        pltpu.make_async_copy(src, dst, in_s.at[i])
        for i, (src, dst) in enumerate(
            (
                (prior.at[:, 0], staged.at[:, 0]),
                (obs_value_hbm, obs_value),
                (obs_var_hbm, obs_var),
                (mask_hbm, ice_mask),
                (wind_hbm, wind),
                (prior.at[:, pl.ds(1, 2)], staged.at[:, pl.ds(1, 2)]),
            )
        )
    ]
    for load in loads:
        load.start()

    barrier = pltpu.get_barrier_semaphore()

    def greet(step, carry):
        at = lax.rem(z * 2 + core + lax.rem(step + 7, 15) + 1, 16)
        pl.semaphore_signal(barrier, inc=1, device_id=ring_device(at // 2, at % 2), device_id_type=MESH)
        return carry

    lax.fori_loop(1, 16, greet, 0)
    pl.semaphore_signal(barrier, inc=1, device_id=side_mate, device_id_type=MESH)

    for load in loads:
        load.wait()
    flat_rows[0] = ice_mask[...].astype(F32)
    flat_rows[1] = wind[0].astype(F32)
    flat_rows[2] = wind[1].astype(F32)
    rows = pl.ds(pl.multiple_of(me * RB, RB), RB)
    surface = [obs_value[...].astype(F32), obs_var[...].astype(F32)]
    surface += [flat_rows[f, rows, :] for f in range(FIELDS)]
    send_obs[...] = jnp.concatenate(surface + [jnp.zeros((RB, LANES), F32)], axis=0).astype(BF16)

    pl.semaphore_wait(barrier, 16)

    def remote(src, dst, s_sem, r_sem, device):
        return pltpu.make_async_remote_copy(
            src_ref=src, dst_ref=dst, send_sem=s_sem, recv_sem=r_sem, device_id=device, device_id_type=MESH
        )

    def settle(ref, sem):
        pltpu.make_async_copy(ref, ref, sem).wait()

    def send_or_keep(same, src, dst, s_sem, r_sem, device):
        @pl.when(same)
        def _():
            pltpu.make_async_copy(src, dst, r_sem).start()

        @pl.when(jnp.logical_not(same))
        def _():
            remote(src, dst, s_sem, r_sem, device).start()

    def wait_sent(same, src, s_sem):
        @pl.when(jnp.logical_not(same))
        def _():
            settle(src, s_sem)

    owner = ring_device(me, half)
    obs_home = jnp.logical_and(owner[0] == me, owner[1] == tile)
    send_or_keep(obs_home, obs_index, index, ob_s.at[1], ob_r.at[1], owner)
    at_home = core == half
    far_first = (4, 3, 5, 2, 6, 1, 7, 0)
    for step in far_first:
        g = lax.rem(z + step, GROUPS)
        there = ring_device(g, half)
        if step:
            remote(staged.at[:, 0, g], thick.at[1, me], at_s.at[0], at_r.at[me], there).start()
        else:
            send_or_keep(at_home, staged.at[:, 0, g], thick.at[1, me], at_s.at[0], at_r.at[me], there)
    send_or_keep(obs_home, send_obs, obs.at[1], ob_s.at[0], ob_r.at[0], owner)
    mate_slot = 2 * core
    side_slot = 2 - 2 * core
    chips = (z_lo, z_lo + 1 - 2 * (z_lo % 2), z_lo + 2 - 4 * (z_lo // 2), 3 - z_lo)
    apart = (core + half) % 2

    def pass_on(i):
        chip = chips[i] * (1 - apart) + chips[3 - i] * apart
        for c in range(2):
            j = chip * 2 + c
            settle(thick.at[1, j], at_r.at[j])
            remote(thick.at[1, j], thick.at[side_slot, j], b_s.at[0], b_r.at[side_slot, 0], side_mate).start()
            remote(thick.at[1, j], thick.at[mate_slot, j], b_s.at[0], b_r.at[mate_slot, 0], chip_mate).start()

    pass_on(0)
    pass_on(1)

    settle(index, ob_r.at[1])
    cell = index[...].astype(F32)
    cell_row = jnp.floor((cell + 0.5) * (1.0 / SPAN))
    cell_col = cell - SPAN * cell_row
    row_at = iota((16, cell.shape[1]), 0).astype(F32)
    col_at = iota((3 * LANES, cell.shape[1]), 0).astype(F32)
    for p in range(PATCHES):
        rows = (row_at == cell_row[p : p + 1]).astype(F32).astype(BF16)
        cols = (col_at == cell_col[p : p + 1] + float(p * PC)).astype(F32).astype(BF16)
        hits = dot_lanes(rows, cols)
        for s in range(3):
            count[s, p] = hits[:RB, s * LANES : (s + 1) * LANES]

    pass_on(2)
    settle(obs.at[1], ob_r.at[0])
    remote(obs.at[1], obs.at[side_slot], b_s.at[1], b_r.at[side_slot, 1], side_mate).start()
    remote(obs.at[1], obs.at[mate_slot], b_s.at[1], b_r.at[mate_slot, 1], chip_mate).start()
    pass_on(3)
    for step in far_first:
        g = lax.rem(z + step, GROUPS)
        there = ring_device(g, half)
        if step:
            remote(staged.at[:, pl.ds(1, 2), g], drift.at[me], ad_s.at[0], ad_r.at[0], there).start()
        else:
            send_or_keep(at_home, staged.at[:, pl.ds(1, 2), g], drift.at[me], ad_s.at[0], ad_r.at[0], there)

    def system_part(s, place):
        both = obs[s].astype(F32)
        values, variance = both[:RB], both[RB : 2 * RB]
        for p in range(PATCHES):
            weight[p * RB : (p + 1) * RB, :] = count[s, p] / variance
        tall[place] = thick[s].astype(F32).reshape(ENS * RB, LANES)

        for pair in range(RB // 2):
            for h in range(2):
                r = pair * 2 + h
                x = tall[place, pl.ds(r, ENS, stride=RB), :]
                mean = jnp.sum(x, axis=0, keepdims=True) * (1.0 / ENS)
                anom = x - mean
                at = (place * RB + r) * LANES
                lanes = slice(at, at + LANES)
                anom_hi[:, lanes], anom_lo[:, lanes] = split(anom)
                pull = weight[pl.ds(r, PATCHES, stride=RB), :] * (values[r : r + 1] - mean)
                pull_high = pull.astype(BF16).astype(F32)
                pulls[:, lanes] = jnp.concatenate([pull_high, pull - pull_high], axis=0).astype(BF16)
                for p in range(PATCHES):
                    row = p * RB + r
                    high, low = split(anom * weight[row : row + 1, :])
                    heavy[p * ENS : (p + 1) * ENS, lanes] = high
                    heavy_lo[p * ENS : (p + 1) * ENS, lanes] = low
            at = (place * RB + pair * 2) * LANES
            span = slice(at, at + 2 * LANES)
            main = dot_lanes(jnp.concatenate([anom_hi[:, span], anom_lo[:, span]], axis=0), heavy[:, span])
            part = main[:ENS] + main[ENS:] + dot_lanes(anom_hi[:, span], heavy_lo[:, span])
            drawn = dot_lanes(pulls[:, span], anom_hi[:, span]) + dot_lanes(pulls[:, span], anom_lo[:, span])
            drawn = drawn[:PATCHES] + drawn[PATCHES:]
            if place == 0 and pair == 0:
                acc[...] = part
                projected[...] = drawn
            else:
                acc[...] += part
                projected[...] += drawn

    system_part(1, 0)

    edge_lane = iota((ENS, LANES), 1)

    def spread(v):
        for r in range(RB):
            j = v * RB + r
            x = tall[v, pl.ds(r, ENS, stride=RB), :]
            part, at = j // 16, j % 16
            for side, shift in ((0, 8 * at), (1, 8 * at + 8)):
                moved = pltpu.roll(x, shift % LANES, 1)
                held = packed[side, part] if at else 0.0
                packed[side, part] = jnp.where(edge_lane // HALO == 2 * at + side, moved, held)
            for p in range(PATCHES):
                masked[p * ENS : (p + 1) * ENS, j * LANES : (j + 1) * LANES] = jnp.where(
                    edge_lane // PC == p, x, 0.0
                ).astype(BF16)

    spread(0)

    def member_device(step):
        to = lax.rem(me + step, GROUPS)
        return to, (to, ring * 2 + core)

    for place, s in ((1, 2 - 2 * core), (2, 2 * core)):
        settle(obs.at[s], b_r.at[s, 1])
        settle(thick.at[s], b_r.at[s, 0])
        system_part(s, place)

    own_lanes = iota((PATCHES, WIDE), 1) // ENS == iota((PATCHES, WIDE), 0)
    drawn = jnp.where(own_lanes, jnp.concatenate([projected[...]] * PATCHES, axis=1), 0.0)
    drawn = jnp.broadcast_to(jnp.sum(drawn, axis=0, keepdims=True), (16, WIDE))
    weights = root_weights(acc[...], drawn)
    left = jnp.concatenate(split(weights), axis=0)

    for v in range(FIELDS):
        if v == 1:
            settle(drift, ad_r.at[0])
            for f in (1, 2):
                tall[f] = drift[:, :, f - 1].astype(F32).reshape(ENS * RB, LANES)
                spread(f)
            for side, p in ((0, 0), (1, PATCHES - 1)):
                edge = dot(left[:, p * ENS : (p + 1) * ENS], jnp.concatenate([packed[side, 0], packed[side, 1]], axis=1).astype(BF16))
                edge_send[side] = (edge[:ENS] + edge[ENS:]).astype(BF16)
            remote(edge_send.at[1 - core], edge_recv.at[core], n_s.at[0], n_r.at[0], chip_mate).start()
            remote(edge_send.at[core], edge_recv.at[1 - core], n_s.at[0], n_r.at[0], side_mate).start()
        for pair in range(RB // 2):
            at = (v * RB + pair * 2) * LANES
            got = dot(left, masked[:, at : at + 256])
            got = got[:ENS] + got[ENS:]
            for to in range(GROUPS):
                rows = slice(to * 8, to * 8 + 8)
                send_c[v, to, pair * 16 : pair * 16 + 16, :] = jnp.concatenate(
                    [got[rows, :LANES], got[rows, LANES:]], axis=0
                ).astype(BF16)
        for step in far_first:
            to, there = member_device(step)
            if step:
                remote(send_c.at[v, to], recv_c.at[v, aligned(EDGE_ROWS * 8 + z * 64, 64, 16)], c_s.at[0], c_r.at[v], there).start()
            else:
                send_or_keep(at_home, send_c.at[v, to], recv_c.at[v, aligned(EDGE_ROWS * 8 + z * 64, 64, 16)], c_s.at[0], c_r.at[v], there)
    at_lane = iota((8, LANES), 1)

    def strip_edges(part, at, q):
        return jnp.where(at_lane // 8 == 4 * q + 1, pltpu.roll(part, (32 * q + 8 - 8 * at) % LANES, 1), 0.0)

    pick_row, pick_lane = iota((4 * LANES, LANES), 0), iota((4 * LANES, LANES), 1)
    pick_col, pick_in = pick_row % LANES, pick_lane % 32
    wanted = jnp.where(pick_in < 8, 120 + pick_in, jnp.where(jnp.logical_and(pick_in >= 16, pick_in < 24), pick_in - 16, -1))
    picks = jnp.logical_and(pick_row // LANES == pick_lane // 32, pick_col == wanted).astype(F32).astype(BF16)

    none = jnp.zeros((8, LANES), F32)
    for ref in (field_x, field_y, normal_x, normal_y, shear):
        ref[0:8, :] = none
        ref[(ROWS + 1) * 8 :, :] = none
    for ref in (strip_x, strip_y, strip_normal_x, strip_normal_y, strip_shear):
        ref[0:8, :] = none
        ref[(STRIP_ROWS + 1) * 8 :, :] = none
    for v in range(FIELDS):
        recv_c[v, 0 : EDGE_ROWS * 8, :] = jnp.zeros((EDGE_ROWS * 8, LANES), BF16)
        recv_c[v, (EDGE_ROWS + ROWS) * 8 :, :] = jnp.zeros((EDGE_ROWS * 8, LANES), BF16)

    for f, (ref, gain) in enumerate(((free, 1.0 / 1.5), (tau_x, 0.5), (tau_y, 0.5))):
        whole = flat_rows[f]
        for row in range(ROWS):
            ref[row * 8 : row * 8 + 8, :] = jnp.broadcast_to(whole[row : row + 1] * gain, (8, LANES))
        padded[0:8, :] = jnp.zeros((8, LANES), F32)
        padded[8 + ROWS :, :] = jnp.zeros((8, LANES), F32)
        padded[8 : 8 + ROWS, :] = whole
        parts = [padded[4 + 16 * q : 4 + 16 * q + STRIP_ROWS, :].astype(BF16) for q in range(4)]
        flat_own[f] = dot(jnp.concatenate(parts, axis=1), picks)

    settle(edge_recv, n_r.at[0])
    merged = edge_recv[0].astype(F32) + edge_recv[1].astype(F32)
    surface = jnp.zeros((RB, LANES), F32)
    for f in range(FIELDS):
        rows = slice((f + 2) * RB, (f + 3) * RB)
        for side, s, shift in ((0, 2, 64 + 8 * f), (1, 0, 72 + 8 * f)):
            moved = pltpu.roll(obs[s, rows, :].astype(F32), shift, 1)
            surface = jnp.where(at_lane // HALO == 16 + 2 * f + side, moved, surface)
    for to in range(GROUPS):
        rows = slice(to * 8, to * 8 + 8)
        send_e[to] = jnp.concatenate([merged[rows, :LANES], merged[rows, LANES:] + surface], axis=0).astype(BF16)
    for step in far_first:
        to, there = member_device(step)
        if step:
            remote(send_e.at[to], recv_e.at[z], e_s.at[0], e_r.at[0], there).start()
        else:
            send_or_keep(at_home, send_e.at[to], recv_e.at[z], e_s.at[0], e_r.at[0], there)

    def pressure(x):
        return 0.125 * (jnp.maximum(x, 0.0) + jnp.log1p(jnp.exp(-jnp.abs(x))))

    def unpack(v):
        settle(recv_c.at[v, pl.ds(EDGE_ROWS * 8, ROWS * 8)], c_r.at[v])
        main = recv_c[v, EDGE_ROWS * 8 : (EDGE_ROWS + ROWS) * 8, :].astype(F32)
        if v == 0:
            press[...] = pressure(main)
            final[0] = main
        else:
            (field_x, field_y)[v - 1][8 : 8 + ROWS * 8, :] = main

    def write_out(v):
        for j in range(GROUPS):
            for start in range(0, ROWS, 16):
                parts = [final[v, pl.ds((start + h * 8) * 8 + j, 8, stride=8), :] for h in range(2)]
                out[j, v, start : start + 16, :] = jnp.concatenate(parts, axis=0).astype(BF16)

    strip_rows = STRIP_ROWS * 8

    def strip_own(v):
        parts = [recv_c[v, 128 * q : 128 * q + strip_rows, :] for q in range(4)]
        return dot(jnp.concatenate(parts, axis=1), picks)

    unpack(0)
    write_out(0)
    strip_halo[0] = strip_own(0)
    unpack(1)
    strip_halo[1] = strip_own(1)
    settle(recv_e, e_r.at[0])
    edges = [recv_e[g].astype(F32) for g in range(GROUPS)]
    for row in range(STRIP_ROWS):
        for v in range(FIELDS):
            total = none if v == 2 else strip_halo[v, row * 8 : row * 8 + 8, :]
            for q in range(4):
                at = 16 * q - EDGE_ROWS + row
                if 0 <= at < ROWS:
                    j = v * RB + at % RB
                    total = total + strip_edges(edges[at // RB][j // 16 * 8 : j // 16 * 8 + 8], j % 16, q)
            strip_halo[v, row * 8 : row * 8 + 8, :] = total
    for f, (strip_ref, gain) in enumerate(((strip_free, 1.0 / 1.5), (strip_tau_x, 0.5), (strip_tau_y, 0.5))):
        flat_halo[...] = jnp.zeros(flat_halo.shape, F32)
        for q in range(4):
            for g in range(max(0, 2 * q - 1), min(GROUPS, 2 * q + 3)):
                start = 8 + 8 * g - 16 * q + EDGE_ROWS
                flat_halo[start : start + 8, :] += strip_edges(edges[g][8:], 8 + f, q)
        whole = (flat_own[f] + flat_halo[8 : 8 + STRIP_ROWS, :]) * gain
        for row in range(STRIP_ROWS):
            strip_ref[row * 8 : row * 8 + 8, :] = jnp.broadcast_to(whole[row : row + 1], (8, LANES))
    row = iota((strip_rows, LANES), 0) // 8
    group = iota((strip_rows, LANES), 1) // 32
    outside = jnp.logical_or(
        jnp.logical_and(group == 0, row < EDGE_ROWS), jnp.logical_and(group == 3, row >= STRIP_ROWS - EDGE_ROWS)
    )
    strip_press[...] = jnp.where(outside, 0.0, pressure(strip_halo[0]))
    strip_x[8 : 8 + strip_rows, :] = strip_halo[1]
    unpack(2)
    strip_y[8 : 8 + strip_rows, :] = strip_halo[2] + strip_own(2)

    def difference(x):
        return pltpu.roll(x, LANES - 1, 1) - pltpu.roll(x, 1, 1)

    main_refs = (field_x, field_y, normal_x, normal_y, shear, press, free, tau_x, tau_y)
    strip_refs = (
        strip_x, strip_y, strip_normal_x, strip_normal_y, strip_shear, strip_press, strip_free, strip_tau_x, strip_tau_y,
    )
    height = 64
    blocks = [(main_refs, i) for i in range(ROWS * 8 // height)]
    for i in range(strip_rows // height):
        blocks.insert(3 * i + 2, (strip_refs, i))

    for sweep in range(2):
        for refs, i in blocks:
            f_x, f_y, n_x, n_y, s_xy, p_ref = refs[:6]
            up, here, down = (slice(i * height + 8 * k, (i + 1) * height + 8 * k) for k in range(3))
            across_x, across_y = difference(f_x[here, :]), difference(f_y[here, :])
            along_x = f_x[down, :] - f_x[up, :]
            along_y = f_y[down, :] - f_y[up, :]
            p = p_ref[up, :]
            spread = across_x + along_y - 1.0
            skew = 0.25 * (across_x - along_y)
            new = (p * (spread + skew), p * (spread - skew), (0.5 * p) * (along_x + across_y))
            for ref, term in zip((n_x, n_y, s_xy), new):
                ref[here, :] = term if sweep == 0 else 0.5 * ref[here, :] + term
        for refs, i in blocks:
            f_x, f_y, n_x, n_y, s_xy, _, open_ref, t_x, t_y = refs
            up, here, down = (slice(i * height + 8 * k, (i + 1) * height + 8 * k) for k in range(3))
            force_x = difference(n_x[here, :]) + (s_xy[down, :] - s_xy[up, :])
            force_y = difference(s_xy[here, :]) + (n_y[down, :] - n_y[up, :])
            f_x[here, :] = open_ref[up, :] * (f_x[here, :] + t_x[up, :] + 0.25 * force_x)
            f_y[here, :] = open_ref[up, :] * (f_y[here, :] + t_y[up, :] + 0.25 * force_y)

    for v, (ref, strip_ref) in ((1, (field_x, strip_x)), (2, (field_y, strip_y))):
        for row in range(0, ROWS, 4):
            q, at = row // 16, row % 16 + EDGE_ROWS + 1
            main = ref[(row + 1) * 8 : (row + 5) * 8, :]
            edge = strip_ref[at * 8 : at * 8 + 32, :]
            col = iota((32, LANES), 1)
            main = jnp.where(col < HALO, pltpu.roll(edge, (LANES - 32 * q - 16) % LANES, 1), main)
            main = jnp.where(col >= LANES - HALO, pltpu.roll(edge, (120 - 32 * q) % LANES, 1), main)
            final[v, row * 8 : row * 8 + 32, :] = main
        write_out(v)

    settle(thick.at[pl.ds(0, 2)], b_s.at[0])
    settle(obs.at[pl.ds(0, 2)], b_s.at[1])
    settle(edge_send, n_s.at[0])
    for sent, sem in ((thick.at[1], at_s), (drift, ad_s), (recv_e, e_s)):

        @pl.when(at_home)
        def _():
            settle(sent.at[pl.ds(0, GROUPS - 1)], sem.at[0])

        @pl.when(jnp.logical_not(at_home))
        def _():
            settle(sent, sem.at[0])

    @pl.when(at_home)
    def _():
        settle(send_c.at[:, pl.ds(0, GROUPS - 1)], c_s.at[0])

    @pl.when(jnp.logical_not(at_home))
    def _():
        settle(send_c, c_s.at[0])

    wait_sent(obs_home, send_obs, ob_s.at[0])
    wait_sent(obs_home, index, ob_s.at[1])


def body(tiles, background, obs_value, obs_var, obs_index, ice_mask, wind_stress):
    dma = pltpu.SemaphoreType.DMA
    inputs = (background.reshape(8, FIELDS, GROUPS, RB, LANES), obs_value, obs_var, obs_index[0], ice_mask, wind_stress)
    return pl.pallas_call(
        functools.partial(kernel, tiles),
        out_shape=jax.ShapeDtypeStruct(background.shape, BF16),
        in_specs=[pl.BlockSpec(memory_space=pltpu.HBM)] * 6,
        out_specs=pl.BlockSpec(memory_space=pltpu.VMEM),
        scratch_shapes=[
            pltpu.VMEM(obs_value.shape, BF16),
            pltpu.VMEM(obs_var.shape, BF16),
            pltpu.VMEM(ice_mask.shape, jnp.int32),
            pltpu.VMEM(wind_stress.shape, BF16),
            pltpu.VMEM((8, FIELDS, GROUPS, RB, LANES), BF16),
            pltpu.VMEM((3, ENS * RB, LANES), F32),
            pltpu.VMEM((48, LANES), BF16),
            pltpu.VMEM((3, GROUPS, 8, RB, LANES), BF16),
            pltpu.VMEM((GROUPS, 8, 2, RB, LANES), BF16),
            pltpu.VMEM((3, 48, LANES), BF16),
            pltpu.VMEM((PATCHES, obs_index.shape[2]), jnp.int32),
            pltpu.VMEM((3, PATCHES, RB, LANES), F32),
            pltpu.VMEM((PATCHES * RB, LANES), F32),
            pltpu.VMEM((ENS, CELLS), BF16),
            pltpu.VMEM((ENS, CELLS), BF16),
            pltpu.VMEM((16, CELLS), BF16),
            pltpu.VMEM((WIDE, CELLS), BF16),
            pltpu.VMEM((WIDE, CELLS), BF16),
            pltpu.VMEM((ENS, WIDE), F32),
            pltpu.VMEM((PATCHES, ENS), F32),
            pltpu.VMEM((WIDE, FIELDS * RB * LANES), BF16),
            pltpu.VMEM((2, 2, ENS, LANES), F32),
            pltpu.VMEM((2, ENS, 2 * LANES), BF16),
            pltpu.VMEM((2, ENS, 2 * LANES), BF16),
            pltpu.VMEM((FIELDS, GROUPS, 64, LANES), BF16),
            pltpu.VMEM((FIELDS, (ROWS + 2 * EDGE_ROWS) * 8, LANES), BF16),
            pltpu.VMEM((GROUPS, 16, LANES), BF16),
            pltpu.VMEM((GROUPS, 16, LANES), BF16),
            pltpu.VMEM((FIELDS, ROWS, LANES), F32),
            pltpu.VMEM((ROWS + 16, LANES), F32),
            pltpu.VMEM((FIELDS, STRIP_ROWS, LANES), F32),
            pltpu.VMEM((STRIP_ROWS + 16, LANES), F32),
            pltpu.VMEM((FIELDS, STRIP_ROWS * 8, LANES), F32),
            *[pltpu.VMEM((ROWS * 8, LANES), F32)] * 4,
            *[pltpu.VMEM(((ROWS + 2) * 8, LANES), F32)] * 5,
            *[pltpu.VMEM((STRIP_ROWS * 8, LANES), F32)] * 4,
            *[pltpu.VMEM(((STRIP_ROWS + 2) * 8, LANES), F32)] * 5,
            pltpu.VMEM((FIELDS, ROWS * 8, LANES), F32),
            dma((6,)),
            dma((1,)), dma((GROUPS,)),
            dma((1,)), dma((1,)),
            dma((2,)), dma((2,)),
            dma((2,)), dma((3, 2)),
            dma((1,)), dma((1,)),
            dma((1,)), dma((FIELDS,)),
            dma((1,)), dma((1,)),
        ],
        compiler_params=pltpu.CompilerParams(
            collective_id=0, has_side_effects=True, vmem_limit_bytes=50 * 1024 * 1024
        ),
        name="analysis_and_drift",
    )(*[pltpu.with_memory_space_constraint(x, pltpu.HBM) for x in inputs])


def solution(mesh):
    placed = (
        P("mem", None, None, "tile"),
        P("mem", "tile"),
        P("mem", "tile"),
        P("mem", "tile", None),
        P(None, "tile"),
        P(None, None, "tile"),
    )
    return jax.shard_map(
        functools.partial(body, mesh.shape["tile"]),
        mesh=mesh,
        in_specs=placed,
        out_specs=P("mem", None, None, "tile"),
        check_vma=False,
    )
```

```python
import functools

import jax
import jax.numpy as jnp
from jax import lax
from jax.experimental import pallas as pl
from jax.experimental.pallas import tpu as pltpu
from jax.sharding import PartitionSpec as P

F32 = jnp.float32
BF16 = jnp.bfloat16
MESH = pl.DeviceIdType.MESH

ENS = 64
GROUPS = 8
RB = 8
ROWS = 64
PC = 16
W = 128
SPAN = PC + 2 * W
LANES = 128
PATCHES = 8
FIELDS = 3
NS_ITERS = 6
WIDE = PATCHES * ENS
CELLS = 3 * RB * LANES
HALO = 4
EDGE_ROWS = 4
STRIP_ROWS = 16 + 2 * EDGE_ROWS


def iota(shape, axis):
    return lax.broadcasted_iota(jnp.int32, shape, axis)


def aligned(start, size, by):
    return pl.ds(pl.multiple_of(start, by), size)


def split(x):
    high = x.astype(BF16)
    return high, (x - high.astype(F32)).astype(BF16)


def dot(a, b):
    return jnp.dot(a, b, preferred_element_type=F32)


def dot_lanes(a, b):
    return lax.dot_general(a, b, (((1,), (1,)), ((), ())), preferred_element_type=F32)


def block_diagonal(x):
    segment = iota(x.shape, 1) // ENS
    zero = jnp.zeros_like(x)
    return jnp.concatenate([jnp.where(segment == q, x, zero) for q in range(4)], axis=0)


def patch_blocks(right, parts):
    lanes = [slice(half * 256, (half + 1) * 256) for half in range(2)]
    return [[block_diagonal(part[:, at]) for part in split(right)[:parts]] for at in lanes]


def patch_products(left, blocks):
    rows = left.shape[0]
    left_high, left_low = split(left)
    out = []
    for half, parts in enumerate(blocks):
        lanes = slice(half * 256, (half + 1) * 256)
        both = dot(jnp.concatenate([left_high[:, lanes], left_low[:, lanes]], axis=0), parts[0])
        total = both[:rows] + both[rows:]
        if len(parts) == 2:
            total = total + dot(left_high[:, lanes], parts[1])
        out.append(total)
    return jnp.concatenate(out, axis=1)


def root_weights(system, projected):
    row = iota((ENS, WIDE), 0)
    eye = ((iota((ENS, WIDE), 1) % ENS) == row).astype(F32)
    full = system + (ENS - 1.0) * eye
    squares = jnp.sum(full * full, axis=0, keepdims=True)
    own = ((iota((PATCHES, WIDE), 1) // ENS) == iota((PATCHES, WIDE), 0)).astype(F32)
    norm = jnp.sum(own * squares, axis=1, keepdims=True)
    scale = jnp.sqrt(jnp.sum(own * norm, axis=0, keepdims=True))
    centring = eye - 1.0 / ENS
    product = (system + (ENS - 1.0) * centring) / scale
    inverse_root = centring
    for sweep in range(NS_ITERS):
        last = sweep == NS_ITERS - 1
        blocks = patch_blocks(0.5 * (eye - product), 2 if last else 1)
        held = jnp.concatenate(([] if last else [product]) + [inverse_root, projected], axis=0)
        held = held + patch_products(held, blocks)
        if not last:
            product, held = held[:ENS], held[ENS:]
            product = product + patch_products(product, blocks)
        inverse_root, projected = held[:ENS], held[ENS:]
    mean_weight = patch_products(projected, patch_blocks(inverse_root, 2))[:1] / scale
    return jnp.sqrt(ENS - 1.0) * (inverse_root / jnp.sqrt(scale)) + (mean_weight + 1.0 / ENS)


def kernel(
    tiles,
    prior, obs_value_hbm, obs_var_hbm, obs_index, mask_hbm, wind_hbm,
    out,
    obs_value, obs_var, ice_mask, wind,
    staged, tall, send_obs, thick, drift, obs, index,
    count, weight, anom_hi, anom_lo, pulls, heavy, acc, projected,
    masked, packed, edge_send, edge_recv,
    send_c, recv_c, send_e, recv_e,
    flat_rows, padded, flat_own, flat_halo, strip_halo,
    free, tau_x, tau_y, press, field_x, field_y, normal_x, normal_y, shear,
    strip_free, strip_tau_x, strip_tau_y, strip_press, strip_x, strip_y, strip_normal_x, strip_normal_y, strip_shear,
    final,
    in_s, at_s, at_r, ad_s, ad_r, ob_s, ob_r, b_s, b_r, n_s, n_r, c_s, c_r, e_s, e_r,
):
    me, tile = lax.axis_index("mem"), lax.axis_index("tile")
    core, z_lo = me % 2, me // 2
    half, ring = tile % 2, tile // 2
    z = half * 4 + z_lo

    def ring_device(at_z, at_core):
        return ((at_z % 4) * 2 + at_core, ring * 2 + at_z // 4)

    chip_mate = (me + 1 - 2 * core, tile)
    side_mate = (me + 1 - 2 * core, lax.rem(tile + tiles - 2 + 4 * core, tiles))

    loads = [
        pltpu.make_async_copy(src, dst, in_s.at[i])
        for i, (src, dst) in enumerate(
            (
                (prior.at[:, 0], staged.at[:, 0]),
                (obs_value_hbm, obs_value),
                (obs_var_hbm, obs_var),
                (mask_hbm, ice_mask),
                (wind_hbm, wind),
                (prior.at[:, pl.ds(1, 2)], staged.at[:, pl.ds(1, 2)]),
            )
        )
    ]
    for load in loads:
        load.start()

    barrier = pltpu.get_barrier_semaphore()

    def greet(step, carry):
        at = lax.rem(z * 2 + core + lax.rem(step + 7, 15) + 1, 16)
        pl.semaphore_signal(barrier, inc=1, device_id=ring_device(at // 2, at % 2), device_id_type=MESH)
        return carry

    lax.fori_loop(1, 16, greet, 0)
    pl.semaphore_signal(barrier, inc=1, device_id=side_mate, device_id_type=MESH)

    for load in loads:
        load.wait()
    flat_rows[0] = ice_mask[...].astype(F32)
    flat_rows[1] = wind[0].astype(F32)
    flat_rows[2] = wind[1].astype(F32)
    rows = pl.ds(pl.multiple_of(me * RB, RB), RB)
    surface = [obs_value[...].astype(F32), obs_var[...].astype(F32)]
    surface += [flat_rows[f, rows, :] for f in range(FIELDS)]
    send_obs[...] = jnp.concatenate(surface + [jnp.zeros((RB, LANES), F32)], axis=0).astype(BF16)

    pl.semaphore_wait(barrier, 16)

    def remote(src, dst, s_sem, r_sem, device):
        return pltpu.make_async_remote_copy(
            src_ref=src, dst_ref=dst, send_sem=s_sem, recv_sem=r_sem, device_id=device, device_id_type=MESH
        )

    def settle(ref, sem):
        pltpu.make_async_copy(ref, ref, sem).wait()

    def send_or_keep(same, src, dst, s_sem, r_sem, device):
        @pl.when(same)
        def _():
            pltpu.make_async_copy(src, dst, r_sem).start()

        @pl.when(jnp.logical_not(same))
        def _():
            remote(src, dst, s_sem, r_sem, device).start()

    def wait_sent(same, src, s_sem):
        @pl.when(jnp.logical_not(same))
        def _():
            settle(src, s_sem)

    owner = ring_device(me, half)
    obs_home = jnp.logical_and(owner[0] == me, owner[1] == tile)
    send_or_keep(obs_home, obs_index, index, ob_s.at[1], ob_r.at[1], owner)
    at_home = core == half
    far_first = (4, 3, 5, 2, 6, 1, 7, 0)
    for step in far_first:
        g = lax.rem(z + step, GROUPS)
        there = ring_device(g, half)
        if step:
            remote(staged.at[:, 0, g], thick.at[1, me], at_s.at[0], at_r.at[me], there).start()
        else:
            send_or_keep(at_home, staged.at[:, 0, g], thick.at[1, me], at_s.at[0], at_r.at[me], there)
    send_or_keep(obs_home, send_obs, obs.at[1], ob_s.at[0], ob_r.at[0], owner)
    mate_slot = 2 * core
    side_slot = 2 - 2 * core
    chips = (z_lo, z_lo + 1 - 2 * (z_lo % 2), z_lo + 2 - 4 * (z_lo // 2), 3 - z_lo)
    apart = (core + half) % 2

    def pass_on(i):
        chip = chips[i] * (1 - apart) + chips[3 - i] * apart
        for c in range(2):
            j = chip * 2 + c
            settle(thick.at[1, j], at_r.at[j])
            remote(thick.at[1, j], thick.at[side_slot, j], b_s.at[0], b_r.at[side_slot, 0], side_mate).start()
            remote(thick.at[1, j], thick.at[mate_slot, j], b_s.at[0], b_r.at[mate_slot, 0], chip_mate).start()

    pass_on(0)
    pass_on(1)

    settle(index, ob_r.at[1])
    cell = index[...].astype(F32)
    cell_row = jnp.floor((cell + 0.5) * (1.0 / SPAN))
    cell_col = cell - SPAN * cell_row
    row_at = iota((16, cell.shape[1]), 0).astype(F32)
    col_at = iota((3 * LANES, cell.shape[1]), 0).astype(F32)
    for p in range(PATCHES):
        rows = (row_at == cell_row[p : p + 1]).astype(F32).astype(BF16)
        cols = (col_at == cell_col[p : p + 1] + float(p * PC)).astype(F32).astype(BF16)
        hits = dot_lanes(rows, cols)
        for s in range(3):
            count[s, p] = hits[:RB, s * LANES : (s + 1) * LANES]

    pass_on(2)
    settle(obs.at[1], ob_r.at[0])
    remote(obs.at[1], obs.at[side_slot], b_s.at[1], b_r.at[side_slot, 1], side_mate).start()
    remote(obs.at[1], obs.at[mate_slot], b_s.at[1], b_r.at[mate_slot, 1], chip_mate).start()
    pass_on(3)
    for step in far_first:
        g = lax.rem(z + step, GROUPS)
        there = ring_device(g, half)
        if step:
            remote(staged.at[:, pl.ds(1, 2), g], drift.at[me], ad_s.at[0], ad_r.at[0], there).start()
        else:
            send_or_keep(at_home, staged.at[:, pl.ds(1, 2), g], drift.at[me], ad_s.at[0], ad_r.at[0], there)

    def system_part(s, place):
        both = obs[s].astype(F32)
        values, variance = both[:RB], both[RB : 2 * RB]
        for p in range(PATCHES):
            weight[p * RB : (p + 1) * RB, :] = count[s, p] / variance
        tall[place] = thick[s].astype(F32).reshape(ENS * RB, LANES)

        for pair in range(RB // 2):
            for h in range(2):
                r = pair * 2 + h
                x = tall[place, pl.ds(r, ENS, stride=RB), :]
                mean = jnp.sum(x, axis=0, keepdims=True) * (1.0 / ENS)
                anom = x - mean
                at = (place * RB + r) * LANES
                lanes = slice(at, at + LANES)
                anom_hi[:, lanes], anom_lo[:, lanes] = split(anom)
                pull = weight[pl.ds(r, PATCHES, stride=RB), :] * (values[r : r + 1] - mean)
                pull_high = pull.astype(BF16).astype(F32)
                pulls[:, lanes] = jnp.concatenate([pull_high, pull - pull_high], axis=0).astype(BF16)
                for p in range(PATCHES):
                    row = p * RB + r
                    heavy[p * ENS : (p + 1) * ENS, lanes] = (anom * weight[row : row + 1, :]).astype(BF16)
            at = (place * RB + pair * 2) * LANES
            span = slice(at, at + 2 * LANES)
            main = dot_lanes(jnp.concatenate([anom_hi[:, span], anom_lo[:, span]], axis=0), heavy[:, span])
            part = main[:ENS] + main[ENS:]
            drawn = dot_lanes(pulls[:, span], anom_hi[:, span]) + dot_lanes(pulls[:, span], anom_lo[:, span])
            drawn = drawn[:PATCHES] + drawn[PATCHES:]
            if place == 0 and pair == 0:
                acc[...] = part
                projected[...] = drawn
            else:
                acc[...] += part
                projected[...] += drawn

    system_part(1, 0)

    edge_lane = iota((ENS, LANES), 1)

    def spread(v):
        for r in range(RB):
            j = v * RB + r
            x = tall[v, pl.ds(r, ENS, stride=RB), :]
            part, at = j // 16, j % 16
            for side, shift in ((0, 8 * at), (1, 8 * at + 8)):
                moved = pltpu.roll(x, shift % LANES, 1)
                held = packed[side, part] if at else 0.0
                packed[side, part] = jnp.where(edge_lane // HALO == 2 * at + side, moved, held)
            for p in range(PATCHES):
                masked[p * ENS : (p + 1) * ENS, j * LANES : (j + 1) * LANES] = jnp.where(
                    edge_lane // PC == p, x, 0.0
                ).astype(BF16)

    spread(0)

    def member_device(step):
        to = lax.rem(me + step, GROUPS)
        return to, (to, ring * 2 + core)

    for place, s in ((1, 2 - 2 * core), (2, 2 * core)):
        settle(obs.at[s], b_r.at[s, 1])
        settle(thick.at[s], b_r.at[s, 0])
        system_part(s, place)

    own_lanes = iota((PATCHES, WIDE), 1) // ENS == iota((PATCHES, WIDE), 0)
    drawn = jnp.where(own_lanes, jnp.concatenate([projected[...]] * PATCHES, axis=1), 0.0)
    drawn = jnp.broadcast_to(jnp.sum(drawn, axis=0, keepdims=True), (16, WIDE))
    weights = root_weights(acc[...], drawn)
    left = jnp.concatenate(split(weights), axis=0)

    for v in range(FIELDS):
        if v == 1:
            settle(drift, ad_r.at[0])
            for f in (1, 2):
                tall[f] = drift[:, :, f - 1].astype(F32).reshape(ENS * RB, LANES)
                spread(f)
            for side, p in ((0, 0), (1, PATCHES - 1)):
                edge = dot(left[:, p * ENS : (p + 1) * ENS], jnp.concatenate([packed[side, 0], packed[side, 1]], axis=1).astype(BF16))
                edge_send[side] = (edge[:ENS] + edge[ENS:]).astype(BF16)
            remote(edge_send.at[1 - core], edge_recv.at[core], n_s.at[0], n_r.at[0], chip_mate).start()
            remote(edge_send.at[core], edge_recv.at[1 - core], n_s.at[0], n_r.at[0], side_mate).start()
        for pair in range(RB // 2):
            at = (v * RB + pair * 2) * LANES
            got = dot(left, masked[:, at : at + 256])
            got = got[:ENS] + got[ENS:]
            for to in range(GROUPS):
                rows = slice(to * 8, to * 8 + 8)
                send_c[v, to, pair * 16 : pair * 16 + 16, :] = jnp.concatenate(
                    [got[rows, :LANES], got[rows, LANES:]], axis=0
                ).astype(BF16)
        for step in far_first:
            to, there = member_device(step)
            if step:
                remote(send_c.at[v, to], recv_c.at[v, aligned(EDGE_ROWS * 8 + z * 64, 64, 16)], c_s.at[0], c_r.at[v], there).start()
            else:
                send_or_keep(at_home, send_c.at[v, to], recv_c.at[v, aligned(EDGE_ROWS * 8 + z * 64, 64, 16)], c_s.at[0], c_r.at[v], there)
    at_lane = iota((8, LANES), 1)

    def strip_edges(part, at, q):
        return jnp.where(at_lane // 8 == 4 * q + 1, pltpu.roll(part, (32 * q + 8 - 8 * at) % LANES, 1), 0.0)

    pick_row, pick_lane = iota((4 * LANES, LANES), 0), iota((4 * LANES, LANES), 1)
    pick_col, pick_in = pick_row % LANES, pick_lane % 32
    wanted = jnp.where(pick_in < 8, 120 + pick_in, jnp.where(jnp.logical_and(pick_in >= 16, pick_in < 24), pick_in - 16, -1))
    picks = jnp.logical_and(pick_row // LANES == pick_lane // 32, pick_col == wanted).astype(F32).astype(BF16)

    none = jnp.zeros((8, LANES), F32)
    for ref in (field_x, field_y, normal_x, normal_y, shear):
        ref[0:8, :] = none
        ref[(ROWS + 1) * 8 :, :] = none
    for ref in (strip_x, strip_y, strip_normal_x, strip_normal_y, strip_shear):
        ref[0:8, :] = none
        ref[(STRIP_ROWS + 1) * 8 :, :] = none
    for v in range(FIELDS):
        recv_c[v, 0 : EDGE_ROWS * 8, :] = jnp.zeros((EDGE_ROWS * 8, LANES), BF16)
        recv_c[v, (EDGE_ROWS + ROWS) * 8 :, :] = jnp.zeros((EDGE_ROWS * 8, LANES), BF16)

    for f, (ref, gain) in enumerate(((free, 1.0 / 1.5), (tau_x, 0.5), (tau_y, 0.5))):
        whole = flat_rows[f]
        for row in range(ROWS):
            ref[row * 8 : row * 8 + 8, :] = jnp.broadcast_to(whole[row : row + 1] * gain, (8, LANES))
        padded[0:8, :] = jnp.zeros((8, LANES), F32)
        padded[8 + ROWS :, :] = jnp.zeros((8, LANES), F32)
        padded[8 : 8 + ROWS, :] = whole
        parts = [padded[4 + 16 * q : 4 + 16 * q + STRIP_ROWS, :].astype(BF16) for q in range(4)]
        flat_own[f] = dot(jnp.concatenate(parts, axis=1), picks)

    settle(edge_recv, n_r.at[0])
    merged = edge_recv[0].astype(F32) + edge_recv[1].astype(F32)
    surface = jnp.zeros((RB, LANES), F32)
    for f in range(FIELDS):
        rows = slice((f + 2) * RB, (f + 3) * RB)
        for side, s, shift in ((0, 2, 64 + 8 * f), (1, 0, 72 + 8 * f)):
            moved = pltpu.roll(obs[s, rows, :].astype(F32), shift, 1)
            surface = jnp.where(at_lane // HALO == 16 + 2 * f + side, moved, surface)
    for to in range(GROUPS):
        rows = slice(to * 8, to * 8 + 8)
        send_e[to] = jnp.concatenate([merged[rows, :LANES], merged[rows, LANES:] + surface], axis=0).astype(BF16)
    for step in far_first:
        to, there = member_device(step)
        if step:
            remote(send_e.at[to], recv_e.at[z], e_s.at[0], e_r.at[0], there).start()
        else:
            send_or_keep(at_home, send_e.at[to], recv_e.at[z], e_s.at[0], e_r.at[0], there)

    def pressure(x):
        return 0.125 * (jnp.maximum(x, 0.0) + jnp.log1p(jnp.exp(-jnp.abs(x))))

    def unpack(v):
        settle(recv_c.at[v, pl.ds(EDGE_ROWS * 8, ROWS * 8)], c_r.at[v])
        main = recv_c[v, EDGE_ROWS * 8 : (EDGE_ROWS + ROWS) * 8, :].astype(F32)
        if v == 0:
            press[...] = pressure(main)
            final[0] = main
        else:
            (field_x, field_y)[v - 1][8 : 8 + ROWS * 8, :] = main

    def write_out(v):
        for j in range(GROUPS):
            for start in range(0, ROWS, 16):
                parts = [final[v, pl.ds((start + h * 8) * 8 + j, 8, stride=8), :] for h in range(2)]
                out[j, v, start : start + 16, :] = jnp.concatenate(parts, axis=0).astype(BF16)

    strip_rows = STRIP_ROWS * 8

    def strip_own(v):
        parts = [recv_c[v, 128 * q : 128 * q + strip_rows, :] for q in range(4)]
        return dot(jnp.concatenate(parts, axis=1), picks)

    unpack(0)
    write_out(0)
    strip_halo[0] = strip_own(0)
    unpack(1)
    strip_halo[1] = strip_own(1)
    settle(recv_e, e_r.at[0])
    edges = [recv_e[g].astype(F32) for g in range(GROUPS)]
    for row in range(STRIP_ROWS):
        for v in range(FIELDS):
            total = none if v == 2 else strip_halo[v, row * 8 : row * 8 + 8, :]
            for q in range(4):
                at = 16 * q - EDGE_ROWS + row
                if 0 <= at < ROWS:
                    j = v * RB + at % RB
                    total = total + strip_edges(edges[at // RB][j // 16 * 8 : j // 16 * 8 + 8], j % 16, q)
            strip_halo[v, row * 8 : row * 8 + 8, :] = total
    for f, (strip_ref, gain) in enumerate(((strip_free, 1.0 / 1.5), (strip_tau_x, 0.5), (strip_tau_y, 0.5))):
        flat_halo[...] = jnp.zeros(flat_halo.shape, F32)
        for q in range(4):
            for g in range(max(0, 2 * q - 1), min(GROUPS, 2 * q + 3)):
                start = 8 + 8 * g - 16 * q + EDGE_ROWS
                flat_halo[start : start + 8, :] += strip_edges(edges[g][8:], 8 + f, q)
        whole = (flat_own[f] + flat_halo[8 : 8 + STRIP_ROWS, :]) * gain
        for row in range(STRIP_ROWS):
            strip_ref[row * 8 : row * 8 + 8, :] = jnp.broadcast_to(whole[row : row + 1], (8, LANES))
    row = iota((strip_rows, LANES), 0) // 8
    group = iota((strip_rows, LANES), 1) // 32
    outside = jnp.logical_or(
        jnp.logical_and(group == 0, row < EDGE_ROWS), jnp.logical_and(group == 3, row >= STRIP_ROWS - EDGE_ROWS)
    )
    strip_press[...] = jnp.where(outside, 0.0, pressure(strip_halo[0]))
    strip_x[8 : 8 + strip_rows, :] = strip_halo[1]
    unpack(2)
    strip_y[8 : 8 + strip_rows, :] = strip_halo[2] + strip_own(2)

    def difference(x):
        return pltpu.roll(x, LANES - 1, 1) - pltpu.roll(x, 1, 1)

    main_refs = (field_x, field_y, normal_x, normal_y, shear, press, free, tau_x, tau_y)
    strip_refs = (
        strip_x, strip_y, strip_normal_x, strip_normal_y, strip_shear, strip_press, strip_free, strip_tau_x, strip_tau_y,
    )
    height = 64
    blocks = [(main_refs, i) for i in range(ROWS * 8 // height)]
    for i in range(strip_rows // height):
        blocks.insert(3 * i + 2, (strip_refs, i))

    for sweep in range(2):
        for refs, i in blocks:
            f_x, f_y, n_x, n_y, s_xy, p_ref = refs[:6]
            up, here, down = (slice(i * height + 8 * k, (i + 1) * height + 8 * k) for k in range(3))
            across_x, across_y = difference(f_x[here, :]), difference(f_y[here, :])
            along_x = f_x[down, :] - f_x[up, :]
            along_y = f_y[down, :] - f_y[up, :]
            p = p_ref[up, :]
            spread = across_x + along_y - 1.0
            skew = 0.25 * (across_x - along_y)
            new = (p * (spread + skew), p * (spread - skew), (0.5 * p) * (along_x + across_y))
            for ref, term in zip((n_x, n_y, s_xy), new):
                ref[here, :] = term if sweep == 0 else 0.5 * ref[here, :] + term
        for refs, i in blocks:
            f_x, f_y, n_x, n_y, s_xy, _, open_ref, t_x, t_y = refs
            up, here, down = (slice(i * height + 8 * k, (i + 1) * height + 8 * k) for k in range(3))
            force_x = difference(n_x[here, :]) + (s_xy[down, :] - s_xy[up, :])
            force_y = difference(s_xy[here, :]) + (n_y[down, :] - n_y[up, :])
            f_x[here, :] = open_ref[up, :] * (f_x[here, :] + t_x[up, :] + 0.25 * force_x)
            f_y[here, :] = open_ref[up, :] * (f_y[here, :] + t_y[up, :] + 0.25 * force_y)

    for v, (ref, strip_ref) in ((1, (field_x, strip_x)), (2, (field_y, strip_y))):
        for row in range(0, ROWS, 4):
            q, at = row // 16, row % 16 + EDGE_ROWS + 1
            main = ref[(row + 1) * 8 : (row + 5) * 8, :]
            edge = strip_ref[at * 8 : at * 8 + 32, :]
            col = iota((32, LANES), 1)
            main = jnp.where(col < HALO, pltpu.roll(edge, (LANES - 32 * q - 16) % LANES, 1), main)
            main = jnp.where(col >= LANES - HALO, pltpu.roll(edge, (120 - 32 * q) % LANES, 1), main)
            final[v, row * 8 : row * 8 + 32, :] = main
        write_out(v)

    settle(thick.at[pl.ds(0, 2)], b_s.at[0])
    settle(obs.at[pl.ds(0, 2)], b_s.at[1])
    settle(edge_send, n_s.at[0])
    for sent, sem in ((thick.at[1], at_s), (drift, ad_s), (recv_e, e_s)):

        @pl.when(at_home)
        def _():
            settle(sent.at[pl.ds(0, GROUPS - 1)], sem.at[0])

        @pl.when(jnp.logical_not(at_home))
        def _():
            settle(sent, sem.at[0])

    @pl.when(at_home)
    def _():
        settle(send_c.at[:, pl.ds(0, GROUPS - 1)], c_s.at[0])

    @pl.when(jnp.logical_not(at_home))
    def _():
        settle(send_c, c_s.at[0])

    wait_sent(obs_home, send_obs, ob_s.at[0])
    wait_sent(obs_home, index, ob_s.at[1])


def body(tiles, background, obs_value, obs_var, obs_index, ice_mask, wind_stress):
    dma = pltpu.SemaphoreType.DMA
    inputs = (background.reshape(8, FIELDS, GROUPS, RB, LANES), obs_value, obs_var, obs_index[0], ice_mask, wind_stress)
    return pl.pallas_call(
        functools.partial(kernel, tiles),
        out_shape=jax.ShapeDtypeStruct(background.shape, BF16),
        in_specs=[pl.BlockSpec(memory_space=pltpu.HBM)] * 6,
        out_specs=pl.BlockSpec(memory_space=pltpu.VMEM),
        scratch_shapes=[
            pltpu.VMEM(obs_value.shape, BF16),
            pltpu.VMEM(obs_var.shape, BF16),
            pltpu.VMEM(ice_mask.shape, jnp.int32),
            pltpu.VMEM(wind_stress.shape, BF16),
            pltpu.VMEM((8, FIELDS, GROUPS, RB, LANES), BF16),
            pltpu.VMEM((3, ENS * RB, LANES), F32),
            pltpu.VMEM((48, LANES), BF16),
            pltpu.VMEM((3, GROUPS, 8, RB, LANES), BF16),
            pltpu.VMEM((GROUPS, 8, 2, RB, LANES), BF16),
            pltpu.VMEM((3, 48, LANES), BF16),
            pltpu.VMEM((PATCHES, obs_index.shape[2]), jnp.int32),
            pltpu.VMEM((3, PATCHES, RB, LANES), F32),
            pltpu.VMEM((PATCHES * RB, LANES), F32),
            pltpu.VMEM((ENS, CELLS), BF16),
            pltpu.VMEM((ENS, CELLS), BF16),
            pltpu.VMEM((16, CELLS), BF16),
            pltpu.VMEM((WIDE, CELLS), BF16),
            pltpu.VMEM((ENS, WIDE), F32),
            pltpu.VMEM((PATCHES, ENS), F32),
            pltpu.VMEM((WIDE, FIELDS * RB * LANES), BF16),
            pltpu.VMEM((2, 2, ENS, LANES), F32),
            pltpu.VMEM((2, ENS, 2 * LANES), BF16),
            pltpu.VMEM((2, ENS, 2 * LANES), BF16),
            pltpu.VMEM((FIELDS, GROUPS, 64, LANES), BF16),
            pltpu.VMEM((FIELDS, (ROWS + 2 * EDGE_ROWS) * 8, LANES), BF16),
            pltpu.VMEM((GROUPS, 16, LANES), BF16),
            pltpu.VMEM((GROUPS, 16, LANES), BF16),
            pltpu.VMEM((FIELDS, ROWS, LANES), F32),
            pltpu.VMEM((ROWS + 16, LANES), F32),
            pltpu.VMEM((FIELDS, STRIP_ROWS, LANES), F32),
            pltpu.VMEM((STRIP_ROWS + 16, LANES), F32),
            pltpu.VMEM((FIELDS, STRIP_ROWS * 8, LANES), F32),
            *[pltpu.VMEM((ROWS * 8, LANES), F32)] * 4,
            *[pltpu.VMEM(((ROWS + 2) * 8, LANES), F32)] * 5,
            *[pltpu.VMEM((STRIP_ROWS * 8, LANES), F32)] * 4,
            *[pltpu.VMEM(((STRIP_ROWS + 2) * 8, LANES), F32)] * 5,
            pltpu.VMEM((FIELDS, ROWS * 8, LANES), F32),
            dma((6,)),
            dma((1,)), dma((GROUPS,)),
            dma((1,)), dma((1,)),
            dma((2,)), dma((2,)),
            dma((2,)), dma((3, 2)),
            dma((1,)), dma((1,)),
            dma((1,)), dma((FIELDS,)),
            dma((1,)), dma((1,)),
        ],
        compiler_params=pltpu.CompilerParams(
            collective_id=0, has_side_effects=True, vmem_limit_bytes=50 * 1024 * 1024
        ),
        name="analysis_and_drift",
    )(*[pltpu.with_memory_space_constraint(x, pltpu.HBM) for x in inputs])


def solution(mesh):
    placed = (
        P("mem", None, None, "tile"),
        P("mem", "tile"),
        P("mem", "tile"),
        P("mem", "tile", None),
        P(None, "tile"),
        P(None, None, "tile"),
    )
    return jax.shard_map(
        functools.partial(body, mesh.shape["tile"]),
        mesh=mesh,
        in_specs=placed,
        out_specs=P("mem", None, None, "tile"),
        check_vma=False,
    )
```
